32 devices in a mesh: parts: 1, basis: 32 (over z, y, x, core).
Axes of the slice: x: 2, y: 2, z: 4, core: 2. Of those that a mesh axis runs over, the one named last changes fastest.
Arguments:
- coulomb: bfloat16 [64, 32, 8, 1024], P(('parts', 'basis')), may hold values from -0.625 to 0.625
- occ_tiles: bfloat16 [32, 2, 1024], P(('parts', 'basis')), may hold values from -0.75 to 0.75
- virt_tiles: bfloat16 [32, 2, 1024], P(('parts', 'basis')), may hold values from -0.75 to 0.75
- tile_count: int32 [32], replicated, may hold values from 1 to 8, 128 in all
- tile_col: int32 [32, 8], replicated, may hold values from 0 to 31, as said below
- dens_col: int32 [32, 2], replicated, may hold values from 0 to 31, as said below
Outputs:
- chi: float32 [64, 64], P(('parts', 'basis'))
The draws below stay inside these ranges and needn't reach their ends.
Inputs may be any that keep to these rules, and one draw needn't show every extreme that they name: `tile_count`: 128 live tiles in all, at most 8 in one block row. `tile_col`: the blocks of one row are distinct. `dens_col`: the blocks of one row are distinct.
All inputs are finite; a program needn't handle non-finite values.
Results may differ from the reference program's by a relative error of at most 0.0042.
Values may be sent and summed in bfloat16 or wider, within the bound.
No kernel may reach another device: no remote copies, remote signals or barrier semaphores. Data moves between devices by JAX's collectives and lax.ppermute only.
A program may use at most 64 MiB of HBM per device.

```python
import math
import jax
import jax.numpy as jnp
import numpy as np
from jax import lax

BW = 32
K = 8
J = 2
AUX = 64
NBLK = 32
LIVE = 128


def local_offsets(key, spread, picked):
    keys = jax.random.split(key, NBLK)
    shuffled = jax.vmap(lambda single: jax.random.permutation(single, 2 * spread + 1))(keys)
    offsets = shuffled[:, :picked].astype(jnp.int32) - spread
    return ((jnp.arange(NBLK, dtype=jnp.int32)[:, None] + offsets) % NBLK).astype(jnp.int32)


def draw_tile_col(key, part):
    key = jax.random.fold_in(key, 11)
    return local_offsets(key, K, K)


def draw_dens_col(key, part):
    key = jax.random.fold_in(key, 13)
    return local_offsets(key, J, J)


def block_levels(own_key, dims, shards, least, high):
    gain, own = 1.0, jax.random.fold_in(own_key, 6)
    for dim, parts in shards:
        steps = jnp.exp(jax.random.uniform(jax.random.fold_in(own, dim), (parts,), jnp.float32, least / len(shards), high / len(shards)))
        gain = gain * jnp.repeat(steps, dims[dim] // parts).reshape([-1 if axis == dim else 1 for axis in range(len(dims))])
    return gain


def profile(count, total, limit, lean):
    loads = [(1 << 20) // math.isqrt(grade ** lean) + 1 for grade in range(2, count + 1)]
    spare, holding = total - limit - (count - 1), [1] * (count - 1)
    while spare > 0:
        candidates = [i for i in range(count - 1) if holding[i] < limit]
        pool, left = sum([loads[i] for i in candidates]), spare
        for i in candidates:
            addition = min(limit - holding[i], max(1, left * loads[i] // pool), spare)
            holding[i] = holding[i] + addition
            spare = spare - addition
    return np.array([limit] + holding)


def ragged(key, amount, total, limit, lean):
    if amount == 2:
        one = jax.random.randint(key, (), max(1, total - limit), min(limit, total - 1) + 1)
        return jnp.stack([one, total - one])
    sizes = jnp.asarray(profile(amount, total, limit, lean), jnp.int32)
    pairs = (amount - 1) // 2
    donor, taker = sizes[1:1 + 2 * pairs:2], sizes[2:2 + 2 * pairs:2]
    margin = jnp.minimum(donor - 1, limit - taker)
    shifted = jax.random.randint(jax.random.fold_in(key, 1), (pairs,), 0, 1 << 20) % (margin + 1)
    sizes = sizes.at[1:1 + 2 * pairs:2].set(donor - shifted).at[2:2 + 2 * pairs:2].set(taker + shifted)
    return sizes[jax.random.permutation(jax.random.fold_in(key, 2), amount)]


def gaussian(own_key, extent, deviation, most, shards=(), kind=jnp.bfloat16):
    result = deviation * jax.random.normal(own_key, extent, jnp.float32)
    if shards:
        result = result * block_levels(own_key, extent, shards, -0.22, 0.18)
    return jnp.clip(result, -most, most).astype(kind)


def setup_inputs(seed: int = 0, part: int = 0) -> dict:
    key_of = jax.random.split(jax.random.key(seed), 7)
    own_keys = jax.random.split(jax.random.fold_in(key_of[6], part), 7)
    coulomb = gaussian(own_keys[0], (AUX, NBLK, K, BW * BW), (2 * (LIVE * BW * BW) ** -0.25), 0.625, ((0, 32),))
    occ_tiles = gaussian(own_keys[1], (NBLK, J, BW * BW), (J * BW) ** -0.5, 0.75, ((0, 32),))
    virt_tiles = gaussian(own_keys[2], (NBLK, J, BW * BW), (J * BW) ** -0.5, 0.75, ((0, 32),))
    tile_count = ragged(key_of[3], NBLK, LIVE, K, 2).astype(jnp.int32)
    tile_col = draw_tile_col(jax.random.fold_in(key_of[6], 71), part)
    dens_col = draw_dens_col(jax.random.fold_in(key_of[6], 71), part)
    return dict(coulomb=coulomb, occ_tiles=occ_tiles, virt_tiles=virt_tiles, tile_count=tile_count, tile_col=tile_col, dens_col=dens_col)


def fetch_tiles(coulomb, live_slot, tile_col, source, wanted):
    candidate = tile_col[source]
    matched = (candidate == wanted[..., None]) & live_slot[source]
    chosen = jnp.sum(jnp.where(matched, jnp.arange(K, dtype=jnp.int32), 0), axis=-1).astype(jnp.int32)
    located = jnp.any(matched, axis=-1)
    taken = coulomb[:, source, chosen].astype(jnp.float32)
    taken = jnp.where(located[None, ..., None], taken, jnp.zeros((), jnp.float32))
    return taken.reshape(taken.shape[:-1] + (BW, BW))


def reference(coulomb, occ_tiles, virt_tiles, tile_count, tile_col, dens_col):
    live_slot = jnp.arange(K, dtype=jnp.int32)[None, :] < tile_count[:, None]
    group = 16 if NBLK % 16 == 0 else 1

    def block_terms(total, block_rows):
        count = block_rows.shape[0]
        columns = tile_col[block_rows]
        partners = dens_col[block_rows]
        full_shape = (count, K, J)
        source = jnp.broadcast_to(partners[:, None, :], full_shape)
        wanted = jnp.broadcast_to(columns[:, :, None], full_shape)
        selected = fetch_tiles(coulomb, live_slot, tile_col, source, wanted)
        density = occ_tiles[block_rows].astype(jnp.float32).reshape(count, J, BW, BW)
        m_occ = jnp.einsum('ajlm,pakjmn->pakln', density, selected).astype(jnp.bfloat16)
        own_rows = jnp.broadcast_to(block_rows[:, None, None], full_shape)
        targets = dens_col[columns]
        selected = fetch_tiles(coulomb, live_slot, tile_col, own_rows, targets)
        virt_dens = virt_tiles[columns].astype(jnp.float32).reshape(count, K, J, BW, BW)
        m_virt = jnp.einsum('pakjlm,akjmn->pakln', selected, virt_dens).astype(jnp.bfloat16)
        live_mask = live_slot[block_rows].astype(jnp.float32)
        m_virt = m_virt.astype(jnp.float32) * live_mask[None, :, :, None, None]
        return total + jnp.einsum('pakln,qakln->pq', m_occ.astype(jnp.float32), m_virt), None

    groups = jnp.arange(NBLK, dtype=jnp.int32).reshape(NBLK // group, group)
    chi, unused = lax.scan(block_terms, jnp.zeros((AUX, AUX), jnp.float32), groups)
    return chi
```

```python
import functools

import jax
import jax.numpy as jnp
from jax import lax
from jax.experimental import pallas as pl
from jax.experimental.pallas import tpu as pltpu
from jax.sharding import PartitionSpec as P

F32, BF16, I32 = jnp.float32, jnp.bfloat16, jnp.int32
BW = 32
TILE = BW * BW
LANES = 128
PACK = LANES // BW
GROUPS = TILE // LANES
PARAMS = pltpu.CompilerParams(vmem_limit_bytes=48 * 1024 * 1024)


def mm(a, b):
    return jnp.dot(a, b, preferred_element_type=F32)


def mm_nt(a, b):
    return lax.dot_general(a, b, (((1,), (1,)), ((), ())), preferred_element_type=F32)


def iota(shape, dim):
    return lax.broadcasted_iota(I32, shape, dim)


def onehot(mask):
    return jnp.where(mask, 1.0, 0.0).astype(BF16)


def spread_tiles(perm_ref):
    for step in range(GROUPS):
        row = iota((LANES, TILE), 0) + step * LANES
        col = iota((LANES, TILE), 1)
        x, y = row // BW, row % BW
        perm_ref[step * LANES : (step + 1) * LANES, :] = onehot(
            col == y * BW + (x % PACK) * GROUPS + x // PACK
        )


def pack_columns(flat, out_ref, aux_dev, first, per_aux, rows, device):
    chunk = iota((rows, LANES), 1) // BW
    for group in range(GROUPS):
        for aux in range(aux_dev):
            turned = []
            for q in range(PACK):
                begin = aux * per_aux + first + q * rows
                part = flat[begin : begin + rows, group * LANES : (group + 1) * LANES]
                turned.append(pltpu.roll(part, q * BW, 1) if q else part)
            for inner in range(PACK):
                picked = turned[-inner % PACK]
                for place in range(1, PACK):
                    picked = jnp.where(chunk == place, turned[(place - inner) % PACK], picked)
                out_ref[device(PACK * group + inner), aux * rows : (aux + 1) * rows, :] = (
                    picked.astype(BF16)
                )


def prepare_kernel(copies, slots_row, cols_ref, dens_ref, t_ref, xt_ref, a_ref, table_ref, perm_ref,
                   flat, planes, lined, swapped):
    aux_dev, slots, _ = t_ref.shape
    live = table_ref.shape[1]
    cols = cols_ref[...]
    is_live = cols >= 0.0
    row_of = (iota((1, slots), 1) // slots_row).astype(F32)
    before = onehot(iota((slots, slots), 0) < iota((slots, slots), 1))
    counted = mm(jnp.broadcast_to(onehot(is_live), (16, slots)), before)[0:1, :]
    compact = jnp.where(is_live, counted, -1.0)
    keep = onehot(iota((live, slots), 0).astype(F32) == compact)
    sub = iota((LANES, slots), 0)
    facts = jnp.where(sub == 0, row_of, jnp.where(sub == 1, cols, 0.0)).astype(BF16)
    places = jnp.where(sub == 0, compact + 1.0, 0.0).astype(BF16)
    own = mm_nt(keep, facts)
    own_row, own_col = own[:, 0:1], own[:, 1:2]
    wide = iota((live, LANES), 1).astype(F32)
    dens = dens_ref[...]
    col_partner = mm_nt(onehot(own_col == wide), dens)
    row_partner = mm_nt(onehot(own_row == wide), dens)
    own_table = mm_nt(facts, keep)
    table_ref[0:2, :] = own_table[0:2, :].astype(I32)
    virt_pick = []
    for j in range(2):
        virt_pick.append(onehot((own_row == row_of) & (col_partner[:, j : j + 1] == cols)))
        occ_pick = onehot((row_partner[:, j : j + 1] == row_of) & (own_col == cols))
        table_ref[2 + j : 3 + j, :] = mm_nt(places, occ_pick)[0:1, :].astype(I32)
    table_ref[4:8, :] = jnp.zeros((4, live), I32)

    spread_tiles(perm_ref)
    for aux in range(aux_dev):
        swapped[aux * live : (aux + 1) * live, :] = mm(keep, t_ref[aux]).astype(BF16)
    flat[...] = mm(swapped[...], perm_ref[...])
    for copy in range(copies):
        pack_columns(flat, xt_ref, aux_dev, 0, live, live // PACK, lambda n: copy * BW + n)

    lane = iota((LANES, LANES), 0)
    x = lane % BW
    within = onehot(
        iota((LANES, LANES), 1) == lane // BW * BW + (x % PACK) * GROUPS + x // PACK
    )
    for aux in range(aux_dev):
        for group in range(GROUPS):
            span = slice(group * LANES, (group + 1) * LANES)
            lined[:, span] = mm(t_ref[aux, :, span], within).astype(BF16)
        for j in range(2):
            gathered = mm(virt_pick[j], lined[...])
            for group in range(GROUPS):
                planes[pl.ds(j * live * 2 * GROUPS + aux * GROUPS + group, live, stride=2 * GROUPS), :] = (
                    gathered[:, group * LANES : (group + 1) * LANES]
                )
    if aux_dev == 1:
        for group in range(GROUPS):
            planes[pl.ds(GROUPS + group, 2 * live, stride=2 * GROUPS), :] = (
                jnp.zeros((2 * live, LANES), F32)
            )
    half = live * 2 * GROUPS
    for j in range(2):
        a_ref[:, j * LANES : (j + 1) * LANES] = planes[j * half : (j + 1) * half, :].astype(BF16)


def virt_kernel(aux_dev, halves, table_ref, dens_ref, a_ref, perm_ref, xm_ref,
                weights, result, swapped, flat):
    live = table_ref.shape[1]
    blocks = dens_ref.shape[0]
    chunk = iota((GROUPS, LANES), 1) // BW

    def build(e, carry):
        tiles = dens_ref[e].astype(F32)
        for j in range(2):
            tile = tiles[j * GROUPS : (j + 1) * GROUPS, :]
            turned = [tile] + [pltpu.roll(tile, d * BW, 1) for d in range(1, PACK)]
            for i in range(PACK):
                for pair in range(PACK // 2):
                    both = [
                        jnp.where(chunk == i, turned[(i - inner) % PACK], 0.0)
                        for inner in (2 * pair, 2 * pair + 1)
                    ]
                    start = pl.multiple_of(e * 2 * LANES, 2 * LANES) + (
                        j * LANES + i * BW + pair * 2 * GROUPS
                    )
                    weights[pl.ds(start, 2 * GROUPS), :] = jnp.concatenate(both, 0).astype(BF16)
        return carry

    lax.fori_loop(0, blocks, build, 0, unroll=4)

    def multiply(step, carry):
        for inner in range(8):
            s = step * 8 + inner
            start = pl.multiple_of(s * 2 * GROUPS, 2 * GROUPS)
            e = pl.multiple_of(table_ref[1, s] * 2 * LANES, 2 * LANES)
            result[pl.ds(start, 2 * GROUPS), :] = mm(
                a_ref[pl.ds(start, 2 * GROUPS), :], weights[pl.ds(e, 2 * LANES), :]
            )
        return carry

    lax.fori_loop(0, live // 8, multiply, 0)
    for aux in range(aux_dev):
        for group in range(GROUPS):
            swapped[aux * live : (aux + 1) * live, group * LANES : (group + 1) * LANES] = (
                result[pl.ds(aux * GROUPS + group, live, stride=2 * GROUPS), :].astype(BF16)
            )
    flat[...] = mm(swapped[...], perm_ref[...])
    part = live // halves
    for half in range(halves):
        pack_columns(flat, xm_ref, aux_dev, half * part, live, part // PACK,
                     lambda n: half * BW + n)


def by_slot(source_ref, wide, aux_dev, rows, devices, r):
    return jnp.concatenate(
        [wide[pl.ds(aux * rows + r, devices, stride=aux_dev * rows), :] for aux in range(aux_dev)],
        0,
    ).astype(BF16)


def widen(source_ref, wide):
    devices, rows, _ = source_ref.shape
    for d in range(devices):
        wide[d * rows : (d + 1) * rows, :] = source_ref[d].astype(F32)


def occ_kernel(aux_dev, table_ref, place_ref, dens_ref, xt_ref, perm_ref, mo_ref,
               wide, held, tiles, lined, planes, weights):
    devices, rows_all, _ = xt_ref.shape
    rows = rows_all // aux_dev
    blocks = dens_ref.shape[0]
    out_rows, aux, _ = mo_ref.shape
    turn, first = place_ref[0], place_ref[1]

    widen(xt_ref, wide)
    for r in range(rows):
        held[r * aux : (r + 1) * aux, :] = by_slot(xt_ref, wide, aux_dev, rows, devices, r)

    height = dens_ref.shape[1]
    for a in range(blocks):
        tiles[a * height : (a + 1) * height, :] = dens_ref[a].astype(F32)
    for j in range(2):
        for group in range(GROUPS):
            lined[j * blocks : (j + 1) * blocks, group * LANES : (group + 1) * LANES] = (
                tiles[pl.ds(2 * GROUPS + j * GROUPS + group, blocks, stride=height), :].astype(BF16)
            )
    turned_tiles = mm(lined[...], perm_ref[...])
    for j in range(2):
        for group in range(GROUPS):
            planes[pl.ds(j * GROUPS + group, blocks, stride=2 * GROUPS), :] = (
                turned_tiles[j * blocks : (j + 1) * blocks, group * LANES : (group + 1) * LANES]
            )
    chunk8 = iota((GROUPS, LANES), 1) // BW

    def build(a, carry):
        base = pl.multiple_of(a * 2 * GROUPS, 2 * GROUPS)
        for j in range(2):
            tile = planes[pl.ds(base + j * GROUPS, GROUPS), :]
            turned = [tile] + [pltpu.roll(tile, d * BW, 1) for d in range(1, PACK)]
            copies = []
            for inner in range(PACK):
                copy = turned[-inner % PACK]
                for place in range(1, PACK):
                    copy = jnp.where(chunk8 == place, turned[(place - inner) % PACK], copy)
                copies.append(copy)
            block = jnp.concatenate(copies, 0).astype(BF16)
            for place in range(PACK):
                start = pl.multiple_of(a * 2 * LANES, 2 * LANES) + j * LANES + place * BW
                weights[pl.ds(start, BW), :] = block
        return carry

    lax.fori_loop(0, blocks, build, 0, unroll=4)
    chunk = iota((aux, LANES), 1) // BW

    def multiply(r, carry):
        total = jnp.zeros((aux, LANES), F32)
        for q in range(PACK):
            s = first + q * out_rows + r
            parts = []
            for j in range(2):
                found = table_ref[2 + j, s] - 1
                source = jnp.maximum(found, 0)
                place = jnp.where(found < 0, -1, (source // rows + turn) % PACK)
                start = pl.multiple_of(source % rows * aux, aux)
                parts.append(jnp.where(chunk == place, held[pl.ds(start, aux), :].astype(F32), 0.0).astype(BF16))
            a = pl.multiple_of(table_ref[0, s] * 2 * LANES, 2 * LANES)
            product = mm(jnp.concatenate(parts, 1), weights[pl.ds(a, 2 * LANES), :])
            total = jnp.where(chunk == (q + turn) % PACK, product, total)
        mo_ref[r] = total.astype(BF16)
        return carry

    lax.fori_loop(0, out_rows, multiply, 0, unroll=2)


def gram_kernel(aux_dev, mo_ref, xm_ref, out_ref, wide):
    devices, rows_all, _ = xm_ref.shape
    rows = rows_all // aux_dev
    aux = aux_dev * devices
    widen(xm_ref, wide)
    total = jnp.zeros((aux, aux), F32)
    for r in range(rows):
        total = total + mm_nt(mo_ref[r], by_slot(xm_ref, wide, aux_dev, rows, devices, r))
    out_ref[...] = jnp.concatenate(
        [total[aux_i * devices : (aux_i + 1) * devices, :] for aux_i in range(aux_dev)], 1
    )


def sum_kernel(aux_dev, part_ref, out_ref):
    devices, width = part_ref.shape
    aux = aux_dev * devices
    total = jnp.sum(part_ref[...], axis=0, keepdims=True)
    lane, col = iota((width, aux), 0), iota((width, aux), 1)
    for row in range(aux_dev):
        chosen = lane == row * aux + col % aux_dev * devices + col // aux_dev
        out_ref[row : row + 1, :] = jnp.dot(
            jnp.broadcast_to(total, (8, width)),
            jnp.where(chosen, 1.0, 0.0),
            precision=lax.Precision.HIGHEST,
            preferred_element_type=F32,
        )[0:1, :]


def call(kernel, outs, scratch, smem, args, name):
    specs = [
        pl.BlockSpec(memory_space=pltpu.SMEM if i < smem else pltpu.VMEM) for i in range(len(args))
    ]
    out_specs = jax.tree.map(lambda _: pl.BlockSpec(memory_space=pltpu.VMEM), outs)
    return pl.pallas_call(
        kernel,
        out_shape=outs,
        in_specs=specs,
        out_specs=out_specs,
        scratch_shapes=scratch,
        compiler_params=PARAMS,
        name=name,
    )(*args)


def exchange(x):
    return lax.all_to_all(x, "basis", split_axis=0, concat_axis=0, tiled=True)


def body(devices, coulomb, occ_tiles, virt_tiles, tile_count, tile_col, dens_col):
    aux_dev, blocks, slots_row, _ = coulomb.shape
    slots = blocks * slots_row
    live = slots // 2
    halves = devices // BW
    aux = aux_dev * devices
    shape = jax.ShapeDtypeStruct

    own = jnp.concatenate([virt_tiles.reshape(-1, LANES), occ_tiles.reshape(-1, LANES)], 0)
    dens = exchange(jnp.broadcast_to(own[None], (devices,) + own.shape))

    live_slot = jnp.arange(slots_row, dtype=I32)[None, :] < tile_count[:, None]
    cols = jnp.where(live_slot, tile_col, -1).astype(F32).reshape(1, slots)
    partners = jnp.pad(dens_col.T.astype(BF16), ((0, LANES - 2), (0, LANES - blocks)))
    rows_t = live // PACK
    rows_m = live // halves // PACK
    xt, gathered, table, perm = call(
        functools.partial(prepare_kernel, halves, slots_row),
        (
            shape((devices, aux_dev * rows_t, LANES), BF16),
            shape((live * 2 * GROUPS, 2 * LANES), BF16),
            shape((8, live), I32),
            shape((TILE, TILE), BF16),
        ),
        [
            pltpu.VMEM((aux_dev * live, TILE), F32),
            pltpu.VMEM((live * 4 * GROUPS, LANES), F32),
            pltpu.VMEM((slots, TILE), BF16),
            pltpu.VMEM((aux_dev * live, TILE), BF16),
        ],
        0,
        (cols, partners, coulomb.reshape(aux_dev, slots, TILE)),
        "prepare",
    )
    xt = exchange(xt)
    xm = call(
        functools.partial(virt_kernel, aux_dev, halves),
        shape((devices, aux_dev * rows_m, LANES), BF16),
        [
            pltpu.VMEM((blocks * 2 * LANES, LANES), BF16),
            pltpu.VMEM((live * 2 * GROUPS, LANES), F32),
            pltpu.VMEM((aux_dev * live, TILE), BF16),
            pltpu.VMEM((aux_dev * live, TILE), F32),
        ],
        1,
        (table, dens, gathered, perm),
        "virt",
    )
    xm = exchange(xm)
    index = lax.axis_index("basis")
    place = jnp.stack([index % PACK, index // BW * (live // halves)]).astype(I32)
    mo = call(
        functools.partial(occ_kernel, aux_dev),
        shape((rows_m, aux, LANES), BF16),
        [
            pltpu.VMEM((devices * aux_dev * rows_t, LANES), F32),
            pltpu.VMEM((rows_t * aux, LANES), BF16),
            pltpu.VMEM((blocks * 4 * GROUPS, LANES), F32),
            pltpu.VMEM((2 * blocks, TILE), BF16),
            pltpu.VMEM((blocks * 2 * GROUPS, LANES), F32),
            pltpu.VMEM((blocks * 2 * LANES, LANES), BF16),
        ],
        2,
        (table, place, dens, xt, perm),
        "occ",
    )
    part = call(
        functools.partial(gram_kernel, aux_dev),
        shape((devices, aux_dev * aux), F32),
        [pltpu.VMEM((devices * aux_dev * rows_m, LANES), F32)],
        0,
        (mo, xm),
        "gram",
    )
    part = exchange(part)
    return call(
        functools.partial(sum_kernel, aux_dev), shape((aux_dev, aux), F32), [], 0, (part,), "total"
    )


def solution(mesh):
    in_specs = (
        P(("parts", "basis"), None, None, None),
        P(("parts", "basis"), None, None),
        P(("parts", "basis"), None, None),
        P(),
        P(),
        P(),
    )
    out_specs = P(("parts", "basis"), None)
    return jax.shard_map(
        functools.partial(body, mesh.shape["basis"]),
        mesh=mesh,
        in_specs=in_specs,
        out_specs=out_specs,
        check_vma=False,
    )
```

```python
import functools

import jax
import jax.numpy as jnp
from jax import lax
from jax.experimental import pallas as pl
from jax.experimental.pallas import tpu as pltpu
from jax.sharding import PartitionSpec as P

F32, BF16, I32 = jnp.float32, jnp.bfloat16, jnp.int32
BW = 32
TILE = BW * BW
LANES = 128
PACK = LANES // BW
GROUPS = TILE // LANES
NEAR = 8


def mm(a, b):
    return jnp.dot(a, b, preferred_element_type=F32)


def mm_nt(a, b):
    return lax.dot_general(a, b, (((1,), (1,)), ((), ())), preferred_element_type=F32)


def iota(shape, dim):
    return lax.broadcasted_iota(I32, shape, dim)


def onehot(mask):
    return jnp.where(mask, 1.0, 0.0).astype(BF16)


def spread_tiles(perm_ref):
    for step in range(GROUPS):
        row = iota((LANES, TILE), 0) + step * LANES
        col = iota((LANES, TILE), 1)
        x, y = row // BW, row % BW
        perm_ref[step * LANES : (step + 1) * LANES, :] = onehot(
            col == y * BW + (x % PACK) * GROUPS + x // PACK
        )


def pack_columns(flat, out_ref, aux_dev, first, per_aux, rows, device):
    chunk = iota((rows, LANES), 1) // BW
    for group in range(GROUPS):
        for aux in range(aux_dev):
            turned = []
            for q in range(PACK):
                begin = aux * per_aux + first + q * rows
                part = flat[begin : begin + rows, group * LANES : (group + 1) * LANES]
                turned.append(pltpu.roll(part, q * BW, 1) if q else part)
            for inner in range(PACK):
                picked = turned[-inner % PACK]
                for place in range(1, PACK):
                    picked = jnp.where(chunk == place, turned[(place - inner) % PACK], picked)
                out_ref[device(PACK * group + inner), aux * rows : (aux + 1) * rows, :] = (
                    picked.astype(BF16)
                )


def format_kernel(virt_hbm, occ_hbm, out_ref, virt_ref, occ_ref, own, sems):
    fetches = [
        pltpu.make_async_copy(virt_hbm, virt_ref, sems.at[0]),
        pltpu.make_async_copy(occ_hbm, occ_ref, sems.at[1]),
    ]
    for fetch in fetches:
        fetch.start()
    for fetch in fetches:
        fetch.wait()
    virt, occ = virt_ref[...].astype(F32), occ_ref[...].astype(F32)
    for group in range(GROUPS):
        span = slice(group * LANES, (group + 1) * LANES)
        own[pl.ds(group, 2, stride=GROUPS), :] = virt[:, span]
        own[pl.ds(2 * GROUPS + group, 2, stride=GROUPS), :] = occ[:, span]
    own_tiles = own[...].astype(BF16)
    for d in range(out_ref.shape[0]):
        out_ref[d] = own_tiles


def index_slots(count_ref, cols_ref):
    slots_row, blocks = cols_ref.shape
    slots = slots_row * blocks
    raw = jnp.where(iota((slots_row, blocks), 0) < count_ref[...], cols_ref[...], -1).astype(F32)
    raw = jnp.concatenate([raw, jnp.zeros((2 * GROUPS - slots_row, blocks), F32)], 0).astype(BF16)
    slot_row = iota((blocks, slots), 1) // slots_row
    spread = mm(raw, onehot(slot_row == iota((blocks, slots), 0)))[:slots_row, :]
    mine = iota((slots_row, slots), 1) % slots_row == iota((slots_row, slots), 0)
    cols = jnp.sum(jnp.where(mine, spread, 0.0), axis=0, keepdims=True)
    is_live = cols >= 0.0
    before = onehot(iota((slots, slots), 0) < iota((slots, slots), 1))
    counted = mm(jnp.broadcast_to(onehot(is_live), (16, slots)), before)[0:1, :]
    row_of = (iota((1, slots), 1) // slots_row).astype(F32)
    return row_of, cols, jnp.where(is_live, counted, -1.0)


def keep_live(compact, live):
    return onehot(iota((live, compact.shape[1]), 0).astype(F32) == compact)


def start_fetches(pairs, sems):
    fetches = [pltpu.make_async_copy(*pair, sems.at[i]) for i, pair in enumerate(pairs)]
    for fetch in fetches:
        fetch.start()
    return fetches


def prepare_kernel(copies, count_hbm, cols_hbm, dens_hbm, t_hbm, *rest):
    outer = len(rest) - 13
    x_refs, (a_ref, table_ref, perm_ref, count_ref, cols_ref, dens_ref, t_ref, xt_ref, flat, planes,
             lined, swapped, sems) = rest[:outer], rest[outer:]
    fetches = start_fetches(
        ((count_hbm, count_ref), (cols_hbm, cols_ref), (dens_hbm, dens_ref), (t_hbm, t_ref)), sems
    )
    aux_dev, slots, _ = t_ref.shape
    live = table_ref.shape[1]
    blocks = cols_ref.shape[1]
    spread_tiles(perm_ref)
    for fetch in fetches[:3]:
        fetch.wait()
    row_of, cols, compact = index_slots(count_ref, cols_ref)
    keep = keep_live(compact, live)
    fetches[3].wait()
    for aux in range(aux_dev):
        swapped[aux * live : (aux + 1) * live, :] = mm(keep, t_ref[aux]).astype(BF16)
    flat[...] = mm(swapped[...], perm_ref[...])
    me = lax.axis_index("basis")
    for copy in range(copies):
        pack_columns(flat, xt_ref, aux_dev, 0, live, live // PACK, lambda n: (copy * BW + n) ^ me)
    for far, x_ref in enumerate(x_refs):
        x_ref[...] = xt_ref[far * NEAR : (far + 1) * NEAR]

    sub = iota((LANES, slots), 0)
    facts = jnp.where(sub == 0, row_of, jnp.where(sub == 1, cols, 0.0)).astype(BF16)
    places = jnp.where(sub == 0, compact + 1.0, 0.0).astype(BF16)
    own_facts = mm_nt(keep, facts)
    own_row, own_col = own_facts[:, 0:1], own_facts[:, 1:2]
    block = iota((live, blocks), 1).astype(F32)
    table_ref[0:2, :] = mm_nt(facts, keep)[0:2, :].astype(I32)
    virt_pick = []
    for j in range(2):
        partner = dens_ref[j : j + 1, :].astype(F32)
        col_partner, row_partner = (
            jnp.sum(jnp.where(place == block, partner, 0.0), axis=1, keepdims=True)
            for place in (own_col, own_row)
        )
        virt_pick.append(onehot((own_row == row_of) & (col_partner == cols)))
        occ_pick = onehot((row_partner == row_of) & (own_col == cols))
        table_ref[2 + j : 3 + j, :] = mm_nt(places, occ_pick)[0:1, :].astype(I32)
    table_ref[4:8, :] = jnp.zeros((4, live), I32)
    lane = iota((LANES, LANES), 0)
    x = lane % BW
    within = onehot(
        iota((LANES, LANES), 1) == lane // BW * BW + (x % PACK) * GROUPS + x // PACK
    )
    for aux in range(aux_dev):
        for group in range(GROUPS):
            span = slice(group * LANES, (group + 1) * LANES)
            lined[:, span] = mm(t_ref[aux, :, span], within).astype(BF16)
        for j in range(2):
            gathered = mm(virt_pick[j], lined[...])
            for group in range(GROUPS):
                planes[pl.ds(j * live * 2 * GROUPS + aux * GROUPS + group, live, stride=2 * GROUPS), :] = (
                    gathered[:, group * LANES : (group + 1) * LANES]
                )
    if aux_dev == 1:
        for group in range(GROUPS):
            planes[pl.ds(GROUPS + group, 2 * live, stride=2 * GROUPS), :] = (
                jnp.zeros((2 * live, LANES), F32)
            )
    half = live * 2 * GROUPS
    for j in range(2):
        a_ref[:, j * LANES : (j + 1) * LANES] = planes[j * half : (j + 1) * half, :].astype(BF16)


def virt_kernel(aux_dev, halves, table_hbm, dens_hbm, a_hbm, perm_hbm, xm_ref, token_ref,
                table_ref, dens_ref, a_ref, perm_ref, weights, result, swapped, flat, sems):
    fetch_dens, fetch_table, fetch_a, fetch_perm = start_fetches(
        ((dens_hbm, dens_ref), (table_hbm, table_ref), (a_hbm, a_ref), (perm_hbm, perm_ref)), sems
    )
    live = table_ref.shape[1]
    token_ref[...] = jnp.zeros(token_ref.shape, F32)
    blocks, rows, _ = dens_ref.shape
    chunk = iota((GROUPS, LANES), 1) // BW

    def build(e, carry):
        tiles = dens_ref[e, : 2 * GROUPS, :].astype(F32)
        for j in range(2):
            tile = tiles[j * GROUPS : (j + 1) * GROUPS, :]
            turned = [tile] + [pltpu.roll(tile, d * BW, 1) for d in range(1, PACK)]
            for i in range(PACK):
                for pair in range(PACK // 2):
                    both = [
                        jnp.where(chunk == i, turned[(i - inner) % PACK], 0.0)
                        for inner in (2 * pair, 2 * pair + 1)
                    ]
                    start = pl.multiple_of(e * 2 * LANES, 2 * LANES) + (
                        j * LANES + i * BW + pair * 2 * GROUPS
                    )
                    weights[pl.ds(start, 2 * GROUPS), :] = jnp.concatenate(both, 0).astype(BF16)
        return carry

    fetch_dens.wait()
    lax.fori_loop(0, blocks, build, 0, unroll=4)
    fetch_table.wait()
    fetch_a.wait()

    def multiply(step, carry):
        for inner in range(32):
            s = step * 32 + inner
            start = pl.multiple_of(s * 2 * GROUPS, 2 * GROUPS)
            e = pl.multiple_of(table_ref[1, s] * 2 * LANES, 2 * LANES)
            result[pl.ds(start, 2 * GROUPS), :] = mm(
                a_ref[pl.ds(start, 2 * GROUPS), :], weights[pl.ds(e, 2 * LANES), :]
            )
        return carry

    lax.fori_loop(0, live // 32, multiply, 0)
    fetch_perm.wait()
    for aux in range(aux_dev):
        for group in range(GROUPS):
            swapped[aux * live : (aux + 1) * live, group * LANES : (group + 1) * LANES] = (
                result[pl.ds(aux * GROUPS + group, live, stride=2 * GROUPS), :].astype(BF16)
            )
    flat[...] = mm(swapped[...], perm_ref[...])
    part = live // halves
    for half in range(halves):
        pack_columns(flat, xm_ref, aux_dev, half * part, live, part // PACK,
                     lambda n: half * BW + n)


def regroup_kernel(token_ref, *refs):
    sources, targets = refs[:-NEAR], refs[-NEAR:]
    for near in range(NEAR):
        for far, source in enumerate(sources):
            targets[near][far] = source[near]


def by_slot(wide, aux_dev, rows, devices, r):
    return jnp.concatenate(
        [wide[pl.ds(aux * rows + r, devices, stride=aux_dev * rows), :] for aux in range(aux_dev)],
        0,
    )


def widen(source_ref, rows, wide):
    devices = source_ref.shape[0]
    for d in range(devices):
        wide[d * rows : (d + 1) * rows, :] = source_ref[d, :rows, :].astype(F32)


def turn_kernel(token_ref, dens_ref, perm_ref, out_ref, tiles, lined, planes):
    blocks = dens_ref.shape[0]
    for a in range(blocks):
        tiles[a * 2 * GROUPS : (a + 1) * 2 * GROUPS, :] = dens_ref[a, 2 * GROUPS :, :].astype(F32)
    for j in range(2):
        for group in range(GROUPS):
            lined[j * blocks : (j + 1) * blocks, group * LANES : (group + 1) * LANES] = (
                tiles[pl.ds(j * GROUPS + group, blocks, stride=2 * GROUPS), :].astype(BF16)
            )
    turned_tiles = mm(lined[...], perm_ref[...])
    for j in range(2):
        for group in range(GROUPS):
            planes[pl.ds(j * GROUPS + group, blocks, stride=2 * GROUPS), :] = (
                turned_tiles[j * blocks : (j + 1) * blocks, group * LANES : (group + 1) * LANES]
            )
    chunk = iota((GROUPS, LANES), 1) // BW

    def build(tile_index, carry):
        tile = planes[pl.ds(pl.multiple_of(tile_index * GROUPS, GROUPS), GROUPS), :]
        turned = [tile] + [pltpu.roll(tile, d * BW, 1) for d in range(1, PACK)]
        copies = []
        for inner in range(PACK):
            copy = turned[-inner % PACK]
            for place in range(1, PACK):
                copy = jnp.where(chunk == place, turned[(place - inner) % PACK], copy)
            copies.append(copy)
        start = pl.multiple_of(tile_index * BW, BW)
        out_ref[pl.ds(start, BW), :] = jnp.concatenate(copies, 0).astype(BF16)
        return carry

    lax.fori_loop(0, 2 * blocks, build, 0, unroll=8)


def occ_kernel(aux_dev, table_ref, turned_ref, *rest):
    x_refs, (mo_ref, wide, held) = rest[:NEAR], rest[NEAR:]
    far_count = x_refs[0].shape[0]
    devices = far_count * NEAR
    rows = table_ref.shape[1] // PACK
    out_rows, aux, _ = mo_ref.shape
    me = lax.axis_index("basis")
    turn, first = me % PACK, me // BW * (out_rows * PACK)
    for near in range(NEAR):
        for far in range(far_count):
            start = pl.multiple_of((me ^ (far * NEAR + near)) * aux_dev * rows, aux_dev * rows)
            wide[pl.ds(start, aux_dev * rows), :] = x_refs[near][far].astype(F32)
    for r in range(rows):
        row = by_slot(wide, aux_dev, rows, devices, r)
        for steps in range(PACK):
            start = (steps * rows + r) * aux
            held[start : start + aux, :] = (
                pltpu.roll(row, steps * BW, 1) if steps else row
            ).astype(BF16)
    none = PACK * rows
    held[none * aux : (none + 1) * aux, :] = jnp.zeros((aux, LANES), BF16)
    in_chunk = [onehot(iota((aux, LANES), 1) // BW == place) for place in range(PACK)]
    of_chunk = [onehot(iota((2 * BW, LANES), 1) // BW == place) for place in range(PACK)]

    def multiply(r, carry):
        parts, blocks = [], []
        for place in range(PACK):
            s = first + (place + PACK - turn) % PACK * out_rows + r
            for j in range(2):
                found = table_ref[2 + j, s] - 1
                source = jnp.maximum(found, 0)
                target = (2 * place + j) % PACK
                steps = (target + 2 * PACK - source // rows - turn) % PACK
                index = jnp.where(found < 0, none, steps * rows + source % rows)
                start = pl.multiple_of(index * aux, aux)
                parts.append(held[pl.ds(start, aux), :] * in_chunk[target])
            a = pl.multiple_of(table_ref[0, s] * 2 * BW, 2 * BW)
            blocks.append(turned_ref[pl.ds(a, 2 * BW), :] * of_chunk[place])
        left = jnp.concatenate([sum(parts[1:PACK], parts[0]), sum(parts[PACK + 1 :], parts[PACK])], 1)
        mo_ref[r] = mm(left, jnp.concatenate(blocks, 0)).astype(BF16)
        return carry

    lax.fori_loop(0, out_rows, multiply, 0, unroll=4)


def gram_kernel(aux_dev, mo_hbm, xm_ref, out_ref, mo_ref, wide, sem):
    fetch = pltpu.make_async_copy(mo_hbm, mo_ref, sem)
    fetch.start()
    devices, rows_all, _ = xm_ref.shape
    rows = rows_all // aux_dev
    aux = aux_dev * devices
    widen(xm_ref, rows_all, wide)
    fetch.wait()
    total = jnp.zeros((aux, aux), F32)
    for r in range(rows):
        total = total + mm_nt(mo_ref[r], by_slot(wide, aux_dev, rows, devices, r).astype(BF16))
    out_ref[...] = jnp.concatenate(
        [total[aux_i * devices : (aux_i + 1) * devices, :] for aux_i in range(aux_dev)], 1
    )


def sum_kernel(aux_dev, part_ref, out_ref):
    devices, width = part_ref.shape
    aux = aux_dev * devices
    total = jnp.sum(part_ref[...], axis=0, keepdims=True)
    lane, col = iota((width, aux), 0), iota((width, aux), 1)
    for row in range(aux_dev):
        chosen = lane == row * aux + col % aux_dev * devices + col // aux_dev
        out_ref[row : row + 1, :] = jnp.dot(
            jnp.broadcast_to(total, (8, width)),
            jnp.where(chosen, 1.0, 0.0),
            precision=lax.Precision.HIGHEST,
            preferred_element_type=F32,
        )[0:1, :]


def call(kernel, outs, scratch, places, args, name, micros, mib=20):
    spaces = {"s": pltpu.SMEM, "v": pltpu.VMEM, "a": pl.ANY}
    return pl.pallas_call(
        kernel,
        out_shape=outs,
        in_specs=[pl.BlockSpec(memory_space=spaces[place]) for place in places],
        out_specs=jax.tree.map(lambda _: pl.BlockSpec(memory_space=pltpu.VMEM), outs),
        scratch_shapes=scratch,
        compiler_params=pltpu.CompilerParams(vmem_limit_bytes=mib * 1024 * 1024),
        cost_estimate=pl.CostEstimate(flops=micros * 1_000_000_000, bytes_accessed=micros * 3_000_000, transcendentals=0),
        name=name,
    )(*args)


def exchange(x):
    return lax.all_to_all(x, "basis", split_axis=0, concat_axis=0, tiled=True)


def permute(x, devices, step):
    return lax.ppermute(x, "basis", [(i, i ^ step) for i in range(devices)])


def body(devices, coulomb, occ_tiles, virt_tiles, tile_count, tile_col, dens_col):
    aux_dev, blocks, slots_row, _ = coulomb.shape
    slots = blocks * slots_row
    live = slots // 2
    halves = devices // BW
    aux = aux_dev * devices
    rows_t = live // PACK
    rows_m = live // halves // PACK
    shape, vmem, dma = jax.ShapeDtypeStruct, pltpu.VMEM, pltpu.SemaphoreType.DMA

    outer = devices // NEAR
    dens = call(
        format_kernel,
        shape((devices, 4 * GROUPS, LANES), BF16),
        [vmem((2, TILE), BF16), vmem((2, TILE), BF16), vmem((4 * GROUPS, LANES), F32), dma((2,))],
        "aa",
        (virt_tiles.reshape(2, TILE), occ_tiles.reshape(2, TILE)),
        "format",
        1,
        60,
    )
    dens = exchange(dens)
    block = (aux_dev * rows_t, LANES)
    counts = tile_count.reshape(1, blocks)
    tiles = coulomb.reshape(aux_dev, slots, TILE)
    *xt, gathered, table, perm = call(
        functools.partial(prepare_kernel, halves),
        (
            *[shape((NEAR,) + block, BF16)] * outer,
            shape((live * 2 * GROUPS, 2 * LANES), BF16),
            shape((8, live), I32),
            shape((TILE, TILE), BF16),
        ),
        [
            vmem((1, blocks), I32),
            vmem((slots_row, blocks), I32),
            vmem((2, blocks), I32),
            vmem((aux_dev, slots, TILE), BF16),
            vmem((devices,) + block, BF16),
            vmem((aux_dev * live, TILE), F32),
            vmem((live * 4 * GROUPS, LANES), F32),
            vmem((slots, TILE), BF16),
            vmem((aux_dev * live, TILE), BF16),
            dma((4,)),
        ],
        "aaaa",
        (counts, tile_col.T, dens_col.T, tiles),
        "prepare",
        5,
        60,
    )
    for far in range(1, outer):
        xt[far] = permute(xt[far], devices, far * NEAR)
    xm, token = call(
        functools.partial(virt_kernel, aux_dev, halves),
        (shape((devices, aux_dev * rows_m, LANES), BF16), shape((8, LANES), F32)),
        [
            pltpu.SMEM((8, live), I32),
            vmem((devices, 4 * GROUPS, LANES), BF16),
            vmem((live * 2 * GROUPS, 2 * LANES), BF16),
            vmem((TILE, TILE), BF16),
            vmem((blocks * 2 * LANES, LANES), BF16),
            vmem((live * 2 * GROUPS, LANES), F32),
            vmem((aux_dev * live, TILE), BF16),
            vmem((aux_dev * live, TILE), F32),
            dma((4,)),
        ],
        "aaaa",
        (table, dens, gathered, perm),
        "virt",
        100,
        60,
    )
    xm = exchange(xm)
    xt = list(call(
        regroup_kernel,
        (shape((outer,) + block, BF16),) * NEAR,
        [],
        "v" * (outer + 1),
        (token, *xt),
        "regroup",
        1,
    ))
    for near in range(1, NEAR):
        xt[near] = permute(xt[near], devices, near)
    turned = call(
        turn_kernel,
        shape((blocks * 2 * BW, LANES), BF16),
        [
            vmem((blocks * 2 * GROUPS, LANES), F32),
            vmem((2 * blocks, TILE), BF16),
            vmem((blocks * 2 * GROUPS, LANES), F32),
        ],
        "vvv",
        (token, dens, perm),
        "turn",
        1,
    )
    mo = call(
        functools.partial(occ_kernel, aux_dev),
        shape((rows_m, aux, LANES), BF16),
        [
            vmem((devices * aux_dev * rows_t, LANES), F32),
            vmem(((PACK * rows_t + 1) * aux, LANES), BF16),
        ],
        "sv" + "v" * NEAR,
        (table, turned, *xt),
        "occ",
        7,
    )
    part = call(
        functools.partial(gram_kernel, aux_dev),
        shape((devices, aux_dev * aux), F32),
        [
            vmem((rows_m, aux, LANES), BF16),
            vmem((devices * aux_dev * rows_m, LANES), F32),
            dma,
        ],
        "av",
        (mo, xm),
        "gram",
        1,
    )
    part = exchange(part)
    return call(
        functools.partial(sum_kernel, aux_dev), shape((aux_dev, aux), F32), [], "v", (part,), "total", 1
    )


def solution(mesh):
    in_specs = (
        P(("parts", "basis"), None, None, None),
        P(("parts", "basis"), None, None),
        P(("parts", "basis"), None, None),
        P(),
        P(),
        P(),
    )
    out_specs = P(("parts", "basis"), None)
    return jax.shard_map(
        functools.partial(body, mesh.shape["basis"]),
        mesh=mesh,
        in_specs=in_specs,
        out_specs=out_specs,
        check_vma=False,
    )
```

```python
import functools

import jax
import jax.numpy as jnp
from jax import lax
from jax.experimental import pallas as pl
from jax.experimental.pallas import tpu as pltpu
from jax.sharding import PartitionSpec as P

F32, BF16, I32 = jnp.float32, jnp.bfloat16, jnp.int32
BW = 32
TILE = BW * BW
LANES = 128
PACK = LANES // BW
GROUPS = TILE // LANES
NEAR = 8


def mm(a, b):
    return jnp.dot(a, b, preferred_element_type=F32)


def mm_nt(a, b):
    return lax.dot_general(a, b, (((1,), (1,)), ((), ())), preferred_element_type=F32)


def iota(shape, dim):
    return lax.broadcasted_iota(I32, shape, dim)


def onehot(mask):
    return jnp.where(mask, 1.0, 0.0).astype(BF16)


def spread_tiles(perm_ref):
    for step in range(GROUPS):
        row = iota((LANES, TILE), 0) + step * LANES
        col = iota((LANES, TILE), 1)
        x, y = row // BW, row % BW
        perm_ref[step * LANES : (step + 1) * LANES, :] = onehot(
            col == y * BW + (x % PACK) * GROUPS + x // PACK
        )


def pack_columns(flat, out_ref, aux_dev, first, per_aux, rows, device):
    chunk = iota((rows, LANES), 1) // BW
    for group in range(GROUPS):
        for aux in range(aux_dev):
            turned = []
            for q in range(PACK):
                begin = aux * per_aux + first + q * rows
                part = flat[begin : begin + rows, group * LANES : (group + 1) * LANES]
                turned.append(pltpu.roll(part, q * BW, 1) if q else part)
            for inner in range(PACK):
                picked = turned[-inner % PACK]
                for place in range(1, PACK):
                    picked = jnp.where(chunk == place, turned[(place - inner) % PACK], picked)
                out_ref[device(PACK * group + inner), aux * rows : (aux + 1) * rows, :] = (
                    picked.astype(BF16)
                )


def as_rows(tiles, rows_ref):
    for group in range(GROUPS):
        rows_ref[pl.ds(group, 2, stride=GROUPS), :] = tiles[0:2, group * LANES : (group + 1) * LANES]
    return rows_ref[...].astype(BF16)


def format_kernel(virt_hbm, out_ref, virt_ref, rows_ref, sem):
    fetch = pltpu.make_async_copy(virt_hbm, virt_ref, sem)
    fetch.start()
    fetch.wait()
    own = as_rows(virt_ref[...].astype(F32), rows_ref)
    for d in range(out_ref.shape[0]):
        out_ref[d] = own


def index_slots(count_ref, cols_ref):
    slots_row, blocks = cols_ref.shape
    slots = slots_row * blocks
    raw = jnp.where(iota((slots_row, blocks), 0) < count_ref[...], cols_ref[...], -1).astype(F32)
    raw = jnp.concatenate([raw, jnp.zeros((2 * GROUPS - slots_row, blocks), F32)], 0).astype(BF16)
    slot_row = iota((blocks, slots), 1) // slots_row
    spread = mm(raw, onehot(slot_row == iota((blocks, slots), 0)))[:slots_row, :]
    mine = iota((slots_row, slots), 1) % slots_row == iota((slots_row, slots), 0)
    cols = jnp.sum(jnp.where(mine, spread, 0.0), axis=0, keepdims=True)
    is_live = cols >= 0.0
    before = onehot(iota((slots, slots), 0) < iota((slots, slots), 1))
    counted = mm(jnp.broadcast_to(onehot(is_live), (16, slots)), before)[0:1, :]
    row_of = (iota((1, slots), 1) // slots_row).astype(F32)
    return row_of, cols, jnp.where(is_live, counted, -1.0)


def keep_live(compact, live):
    return onehot(iota((live, compact.shape[1]), 0).astype(F32) == compact)


def start_fetches(pairs, sems):
    fetches = [pltpu.make_async_copy(*pair, sems.at[i]) for i, pair in enumerate(pairs)]
    for fetch in fetches:
        fetch.start()
    return fetches


def prepare_kernel(copies, count_hbm, cols_hbm, dens_hbm, occ_hbm, t_hbm, *rest):
    outer = len(rest) - 16
    x_refs, (a_ref, table_ref, perm_hbm, perm_ref, count_ref, cols_ref, dens_ref, occ_ref, t_ref,
             rows_ref, xt_ref, flat, planes, lined, swapped, sems) = rest[:outer], rest[outer:]
    fetches = start_fetches(
        ((count_hbm, count_ref), (cols_hbm, cols_ref), (dens_hbm, dens_ref), (occ_hbm, occ_ref),
         (t_hbm, t_ref)),
        sems,
    )
    aux_dev, slots, _ = t_ref.shape
    live = table_ref.shape[1]
    blocks = cols_ref.shape[1]
    spread_tiles(perm_ref)
    keep_perm = pltpu.make_async_copy(perm_ref, perm_hbm, sems.at[5])
    keep_perm.start()
    for fetch in fetches[:4]:
        fetch.wait()
    occ = jnp.concatenate(
        [occ_ref[...].astype(F32), jnp.zeros((2 * GROUPS - 2, TILE), F32)], 0
    ).astype(BF16)
    own = as_rows(mm(occ, perm_ref[...]), rows_ref)
    row_of, cols, compact = index_slots(count_ref, cols_ref)
    keep = keep_live(compact, live)
    fetches[4].wait()
    for aux in range(aux_dev):
        swapped[aux * live : (aux + 1) * live, :] = mm(keep, t_ref[aux]).astype(BF16)
    flat[...] = mm(swapped[...], perm_ref[...])
    me = lax.axis_index("basis")
    for copy in range(copies):
        pack_columns(flat, xt_ref, aux_dev, 0, live, live // PACK, lambda n: (copy * BW + n) ^ me)
    height = xt_ref.shape[1]
    for far, x_ref in enumerate(x_refs):
        for near in range(NEAR):
            x_ref[near * height : (near + 1) * height, :] = xt_ref[far * NEAR + near]
        x_ref[NEAR * height :, :] = own

    sub = iota((LANES, slots), 0)
    facts = jnp.where(sub == 0, row_of, jnp.where(sub == 1, cols, 0.0)).astype(BF16)
    places = jnp.where(sub == 0, compact + 1.0, 0.0).astype(BF16)
    own_facts = mm_nt(keep, facts)
    own_row, own_col = own_facts[:, 0:1], own_facts[:, 1:2]
    block = iota((live, blocks), 1).astype(F32)
    own_table = mm_nt(facts, keep)[0:2, :].astype(I32)
    table_ref[0:1, :] = own_table[0:1, :] * (2 * BW)
    table_ref[1:2, :] = own_table[1:2, :] * (2 * LANES)
    turn = me % PACK
    part, rows = live // copies, live // PACK
    out_place = ((iota((1, live), 1) + live - me // BW * part) // (part // PACK) + turn) % PACK
    aux = aux_dev * len(x_refs) * NEAR
    virt_pick = []
    for j in range(2):
        partner = dens_ref[j : j + 1, :].astype(F32)
        col_partner, row_partner = (
            jnp.sum(jnp.where(place == block, partner, 0.0), axis=1, keepdims=True)
            for place in (own_col, own_row)
        )
        virt_pick.append(onehot((own_row == row_of) & (col_partner == cols)))
        occ_pick = onehot((row_partner == row_of) & (own_col == cols))
        found = mm_nt(places, occ_pick)[0:1, :].astype(I32) - 1
        source = jnp.maximum(found, 0)
        steps = (out_place * 2 + j + 3 * PACK - source // rows - turn) % PACK
        index = jnp.where(found < 0, PACK * rows, steps * rows + source % rows)
        table_ref[2 + j : 3 + j, :] = index * aux
    table_ref[4:8, :] = jnp.zeros((4, live), I32)
    lane = iota((LANES, LANES), 0)
    x = lane % BW
    within = onehot(
        iota((LANES, LANES), 1) == lane // BW * BW + (x % PACK) * GROUPS + x // PACK
    )
    for aux in range(aux_dev):
        for group in range(GROUPS):
            span = slice(group * LANES, (group + 1) * LANES)
            lined[:, span] = mm(t_ref[aux, :, span], within).astype(BF16)
        for j in range(2):
            gathered = mm(virt_pick[j], lined[...])
            for group in range(GROUPS):
                planes[pl.ds(j * live * 2 * GROUPS + aux * GROUPS + group, live, stride=2 * GROUPS), :] = (
                    gathered[:, group * LANES : (group + 1) * LANES]
                )
    if aux_dev == 1:
        for group in range(GROUPS):
            planes[pl.ds(GROUPS + group, 2 * live, stride=2 * GROUPS), :] = (
                jnp.zeros((2 * live, LANES), F32)
            )
    half = live * 2 * GROUPS
    for j in range(2):
        a_ref[:, j * LANES : (j + 1) * LANES] = planes[j * half : (j + 1) * half, :].astype(BF16)
    keep_perm.wait()


def virt_kernel(aux_dev, halves, table_hbm, dens_ref, a_ref, perm_hbm, xm_ref, token_ref,
                table_ref, perm_ref, weights, result, swapped, flat, sems):
    fetch_table, fetch_perm = start_fetches(((table_hbm, table_ref), (perm_hbm, perm_ref)), sems)
    live = table_ref.shape[1]
    token_ref[...] = jnp.zeros(token_ref.shape, F32)
    blocks, rows, _ = dens_ref.shape
    chunk = iota((GROUPS, LANES), 1) // BW

    def build(e, carry):
        tiles = dens_ref[e].astype(F32)
        for j in range(2):
            tile = tiles[j * GROUPS : (j + 1) * GROUPS, :]
            turned = [tile] + [pltpu.roll(tile, d * BW, 1) for d in range(1, PACK)]
            for i in range(PACK):
                for pair in range(PACK // 2):
                    both = [
                        jnp.where(chunk == i, turned[(i - inner) % PACK], 0.0)
                        for inner in (2 * pair, 2 * pair + 1)
                    ]
                    start = pl.multiple_of(e * 2 * LANES, 2 * LANES) + (
                        j * LANES + i * BW + pair * 2 * GROUPS
                    )
                    weights[pl.ds(start, 2 * GROUPS), :] = jnp.concatenate(both, 0).astype(BF16)
        return carry

    lax.fori_loop(0, blocks, build, 0, unroll=8)
    fetch_table.wait()

    def multiply(step, carry):
        for inner in range(64):
            s = step * 64 + inner
            start = pl.multiple_of(s * 2 * GROUPS, 2 * GROUPS)
            e = pl.multiple_of(table_ref[1, s], 2 * LANES)
            result[pl.ds(start, 2 * GROUPS), :] = mm(
                a_ref[pl.ds(start, 2 * GROUPS), :], weights[pl.ds(e, 2 * LANES), :]
            )
        return carry

    lax.fori_loop(0, live // 64, multiply, 0)
    for aux in range(aux_dev):
        for group in range(GROUPS):
            swapped[aux * live : (aux + 1) * live, group * LANES : (group + 1) * LANES] = (
                result[pl.ds(aux * GROUPS + group, live, stride=2 * GROUPS), :].astype(BF16)
            )
    fetch_perm.wait()
    flat[...] = mm(swapped[...], perm_ref[...])
    part = live // halves
    for half in range(halves):
        pack_columns(flat, xm_ref, aux_dev, half * part, live, part // PACK,
                     lambda n: half * BW + n)


def regroup_kernel(token_ref, *refs):
    sources, targets = refs[:-NEAR], refs[-NEAR:]
    outer = len(sources)
    height = (sources[0].shape[0] - 2 * GROUPS) // NEAR
    for near, target in enumerate(targets):
        for far, source in enumerate(sources):
            target[far * height : (far + 1) * height, :] = (
                source[near * height : (near + 1) * height, :]
            )
            tiles = outer * height + far * 2 * GROUPS
            target[tiles : tiles + 2 * GROUPS, :] = source[NEAR * height :, :]


def by_slot(wide, aux_dev, rows, devices, r):
    return jnp.concatenate(
        [wide[pl.ds(aux * rows + r, devices, stride=aux_dev * rows), :] for aux in range(aux_dev)],
        0,
    )


def widen(source_ref, rows, wide):
    devices = source_ref.shape[0]
    for d in range(devices):
        wide[d * rows : (d + 1) * rows, :] = source_ref[d, :rows, :].astype(F32)


def occ_kernel(aux_dev, table_hbm, *rest):
    x_refs, (mo_ref, table_ref, wide, planes, weights, held, sem) = rest[:NEAR], rest[NEAR:]
    fetch_table = pltpu.make_async_copy(table_hbm, table_ref, sem)
    fetch_table.start()
    rows = table_ref.shape[1] // PACK
    height = aux_dev * rows
    outer = x_refs[0].shape[0] // (height + 2 * GROUPS)
    devices = outer * NEAR
    out_rows, aux, _ = mo_ref.shape
    me = lax.axis_index("basis")
    for near, x_ref in enumerate(x_refs):
        for far in range(outer):
            owner = me ^ (far * NEAR + near)
            wide[pl.ds(pl.multiple_of(owner * height, height), height), :] = (
                x_ref[far * height : (far + 1) * height, :].astype(F32)
            )
            tiles = outer * height + far * 2 * GROUPS
            planes[pl.ds(pl.multiple_of(owner * 2 * GROUPS, 2 * GROUPS), 2 * GROUPS), :] = (
                x_ref[tiles : tiles + 2 * GROUPS, :].astype(F32)
            )
    chunk = iota((GROUPS, LANES), 1) // BW

    def build(tile_index, carry):
        tile = planes[pl.ds(pl.multiple_of(tile_index * GROUPS, GROUPS), GROUPS), :]
        turned = [tile] + [pltpu.roll(tile, d * BW, 1) for d in range(1, PACK)]
        copies = []
        for inner in range(PACK):
            copy = turned[-inner % PACK]
            for place in range(1, PACK):
                copy = jnp.where(chunk == place, turned[(place - inner) % PACK], copy)
            copies.append(copy)
        start = pl.multiple_of(tile_index * BW, BW)
        weights[pl.ds(start, BW), :] = jnp.concatenate(copies, 0).astype(BF16)
        return carry

    lax.fori_loop(0, 2 * devices, build, 0, unroll=8)
    for r in range(rows):
        row = by_slot(wide, aux_dev, rows, devices, r)
        for steps in range(PACK):
            start = (steps * rows + r) * aux
            held[start : start + aux, :] = (
                pltpu.roll(row, steps * BW, 1) if steps else row
            ).astype(BF16)
    none = PACK * rows
    held[none * aux : (none + 1) * aux, :] = jnp.zeros((aux, LANES), BF16)
    in_chunk = [onehot(iota((aux, LANES), 1) // BW == place) for place in range(PACK)]
    of_chunk = [onehot(iota((2 * BW, LANES), 1) // BW == place) for place in range(PACK)]
    first = me // BW * (out_rows * PACK)
    bases = [first + (place + PACK - me % PACK) % PACK * out_rows for place in range(PACK)]
    fetch_table.wait()

    def multiply(r, carry):
        parts, blocks = [], []
        for place in range(PACK):
            s = bases[place] + r
            for j in range(2):
                start = pl.multiple_of(table_ref[2 + j, s], aux)
                parts.append(held[pl.ds(start, aux), :] * in_chunk[(2 * place + j) % PACK])
            a = pl.multiple_of(table_ref[0, s], 2 * BW)
            blocks.append(weights[pl.ds(a, 2 * BW), :] * of_chunk[place])
        left = jnp.concatenate([sum(parts[1:PACK], parts[0]), sum(parts[PACK + 1 :], parts[PACK])], 1)
        mo_ref[r] = mm(left, jnp.concatenate(blocks, 0)).astype(BF16)
        return carry

    lax.fori_loop(0, out_rows, multiply, 0, unroll=8)


def gram_kernel(aux_dev, mo_ref, xm_ref, out_ref, wide):
    devices, rows_all, _ = xm_ref.shape
    rows = rows_all // aux_dev
    aux = aux_dev * devices
    widen(xm_ref, rows_all, wide)
    total = jnp.zeros((aux, aux), F32)
    for r in range(rows):
        total = total + mm_nt(mo_ref[r], by_slot(wide, aux_dev, rows, devices, r).astype(BF16))
    out_ref[...] = jnp.concatenate(
        [total[aux_i * devices : (aux_i + 1) * devices, :] for aux_i in range(aux_dev)], 1
    )


def sum_kernel(aux_dev, part_ref, out_ref):
    devices, width = part_ref.shape
    aux = aux_dev * devices
    total = jnp.sum(part_ref[...], axis=0, keepdims=True)
    lane, col = iota((width, aux), 0), iota((width, aux), 1)
    for row in range(aux_dev):
        chosen = lane == row * aux + col % aux_dev * devices + col // aux_dev
        out_ref[row : row + 1, :] = jnp.dot(
            jnp.broadcast_to(total, (8, width)),
            jnp.where(chosen, 1.0, 0.0),
            precision=lax.Precision.HIGHEST,
            preferred_element_type=F32,
        )[0:1, :]


def is_hbm(out):
    return getattr(out, "memory_space", None) == pltpu.HBM


def call(kernel, outs, scratch, places, args, name, micros, mib=24):
    specs = {"v": pltpu.VMEM, "m": pltpu.VMEM, "a": pl.ANY, "h": pl.ANY}
    held = {"m": pltpu.VMEM, "a": pltpu.VMEM, "h": pltpu.HBM}
    args = [
        pltpu.with_memory_space_constraint(arg, held[place]) if place in held else arg
        for place, arg in zip(places, args)
    ]
    return pl.pallas_call(
        kernel,
        out_shape=outs,
        in_specs=[pl.BlockSpec(memory_space=specs[place]) for place in places],
        out_specs=jax.tree.map(
            lambda out: pl.BlockSpec(memory_space=pl.ANY if is_hbm(out) else pltpu.VMEM), outs
        ),
        scratch_shapes=scratch,
        compiler_params=pltpu.CompilerParams(vmem_limit_bytes=mib * 1024 * 1024),
        cost_estimate=pl.CostEstimate(
            flops=micros * 1_000_000_000, bytes_accessed=micros * 3_000_000, transcendentals=0
        ),
        name=name,
    )(*args)


def exchange(x):
    return lax.all_to_all(x, "basis", split_axis=0, concat_axis=0, tiled=True)


def permute(x, devices, step):
    return lax.ppermute(x, "basis", [(i, i ^ step) for i in range(devices)])


def body(devices, coulomb, occ_tiles, virt_tiles, tile_count, tile_col, dens_col):
    aux_dev, blocks, slots_row, _ = coulomb.shape
    slots = blocks * slots_row
    live = slots // 2
    halves = devices // BW
    aux = aux_dev * devices
    rows_t = live // PACK
    rows_m = live // halves // PACK
    shape, vmem, dma = jax.ShapeDtypeStruct, pltpu.VMEM, pltpu.SemaphoreType.DMA

    outer = devices // NEAR
    dens = call(
        format_kernel,
        shape((devices, 2 * GROUPS, LANES), BF16),
        [vmem((2, TILE), BF16), vmem((2 * GROUPS, LANES), F32), dma],
        "h",
        (virt_tiles.reshape(2, TILE),),
        "format",
        1,
    )
    dens = exchange(dens)
    height = aux_dev * rows_t
    *xt, gathered, table, perm = call(
        functools.partial(prepare_kernel, halves),
        (
            *[shape((NEAR * height + 2 * GROUPS, LANES), BF16)] * outer,
            vmem((live * 2 * GROUPS, 2 * LANES), BF16),
            vmem((8, live), I32),
            pltpu.HBM((TILE, TILE), BF16),
        ),
        [
            vmem((TILE, TILE), BF16),
            vmem((1, blocks), I32),
            vmem((slots_row, blocks), I32),
            vmem((2, blocks), I32),
            vmem((2, TILE), BF16),
            vmem((aux_dev, slots, TILE), BF16),
            vmem((2 * GROUPS, LANES), F32),
            vmem((devices, height, LANES), BF16),
            vmem((aux_dev * live, TILE), F32),
            vmem((live * 4 * GROUPS, LANES), F32),
            vmem((slots, TILE), BF16),
            vmem((aux_dev * live, TILE), BF16),
            dma((6,)),
        ],
        "hhhhh",
        (
            tile_count.reshape(1, blocks),
            tile_col.T,
            dens_col.T,
            occ_tiles.reshape(2, TILE),
            coulomb.reshape(aux_dev, slots, TILE),
        ),
        "prepare",
        5,
    )
    for far in range(1, outer):
        xt[far] = permute(xt[far], devices, far * NEAR)
    xm, token = call(
        functools.partial(virt_kernel, aux_dev, halves),
        (shape((devices, aux_dev * rows_m, LANES), BF16), vmem((8, LANES), F32)),
        [
            pltpu.SMEM((8, live), I32),
            vmem((TILE, TILE), BF16),
            vmem((blocks * 2 * LANES, LANES), BF16),
            vmem((live * 2 * GROUPS, LANES), F32),
            vmem((aux_dev * live, TILE), BF16),
            vmem((aux_dev * live, TILE), F32),
            dma((2,)),
        ],
        "avmh",
        (table, dens, gathered, perm),
        "virt",
        100,
    )
    xm = exchange(xm)
    xt = list(call(
        regroup_kernel,
        (shape((outer * (height + 2 * GROUPS), LANES), BF16),) * NEAR,
        [],
        "m" + "v" * outer,
        (token, *xt),
        "regroup",
        1,
    ))
    for near in range(1, NEAR):
        xt[near] = permute(xt[near], devices, near)
    mo = call(
        functools.partial(occ_kernel, aux_dev),
        vmem((rows_m, aux, LANES), BF16),
        [
            pltpu.SMEM((8, live), I32),
            vmem((devices * height, LANES), F32),
            vmem((devices * 2 * GROUPS, LANES), F32),
            vmem((devices * 2 * BW, LANES), BF16),
            vmem(((PACK * rows_t + 1) * aux, LANES), BF16),
            dma,
        ],
        "a" + "v" * NEAR,
        (table, *xt),
        "occ",
        8,
    )
    part = call(
        functools.partial(gram_kernel, aux_dev),
        shape((devices, aux_dev * aux), F32),
        [
            vmem((devices * aux_dev * rows_m, LANES), F32),
        ],
        "mv",
        (mo, xm),
        "gram",
        1,
    )
    part = exchange(part)
    return call(
        functools.partial(sum_kernel, aux_dev), shape((aux_dev, aux), F32), [], "v", (part,), "total", 1
    )


def solution(mesh):
    in_specs = (
        P(("parts", "basis"), None, None, None),
        P(("parts", "basis"), None, None),
        P(("parts", "basis"), None, None),
        P(),
        P(),
        P(),
    )
    out_specs = P(("parts", "basis"), None)
    return jax.shard_map(
        functools.partial(body, mesh.shape["basis"]),
        mesh=mesh,
        in_specs=in_specs,
        out_specs=out_specs,
        check_vma=False,
    )
```

```python
import functools

import jax
import jax.numpy as jnp
from jax import lax
from jax.experimental import pallas as pl
from jax.experimental.pallas import tpu as pltpu
from jax.sharding import PartitionSpec as P

F32, BF16, I32 = jnp.float32, jnp.bfloat16, jnp.int32
BW = 32
TILE = BW * BW
LANES = 128
PACK = LANES // BW
GROUPS = TILE // LANES
NEAR = 8


def mm(a, b):
    return jnp.dot(a, b, preferred_element_type=F32)


def mm_nt(a, b):
    return lax.dot_general(a, b, (((1,), (1,)), ((), ())), preferred_element_type=F32)


def iota(shape, dim):
    return lax.broadcasted_iota(I32, shape, dim)


def onehot(mask):
    return jnp.where(mask, 1.0, 0.0).astype(BF16)


def spread_tiles(perm_ref):
    for step in range(GROUPS):
        row = iota((LANES, TILE), 0) + step * LANES
        col = iota((LANES, TILE), 1)
        x, y = row // BW, row % BW
        perm_ref[step * LANES : (step + 1) * LANES, :] = onehot(
            col == y * BW + (x % PACK) * GROUPS + x // PACK
        )


def pack_columns(flat, out_ref, aux_dev, first, per_aux, rows, device):
    chunk = iota((rows, LANES), 1) // BW
    for group in range(GROUPS):
        for aux in range(aux_dev):
            turned = []
            for q in range(PACK):
                begin = aux * per_aux + first + q * rows
                part = flat[begin : begin + rows, group * LANES : (group + 1) * LANES]
                turned.append(pltpu.roll(part, q * BW, 1) if q else part)
            for inner in range(PACK):
                picked = turned[-inner % PACK]
                for place in range(1, PACK):
                    picked = jnp.where(chunk == place, turned[(place - inner) % PACK], picked)
                out_ref[device(PACK * group + inner), aux * rows : (aux + 1) * rows, :] = (
                    picked.astype(BF16)
                )


def as_rows(tiles, rows_ref):
    for group in range(GROUPS):
        rows_ref[pl.ds(group, 2, stride=GROUPS), :] = tiles[0:2, group * LANES : (group + 1) * LANES]
    return rows_ref[...].astype(BF16)


def format_kernel(virt_hbm, out_ref, virt_ref, rows_ref, sem):
    fetch = pltpu.make_async_copy(virt_hbm, virt_ref, sem)
    fetch.start()
    fetch.wait()
    own = as_rows(virt_ref[...].astype(F32), rows_ref)
    for d in range(out_ref.shape[0]):
        out_ref[d] = own


def index_slots(count_ref, cols_ref):
    slots_row, blocks = cols_ref.shape
    slots = slots_row * blocks
    raw = jnp.where(iota((slots_row, blocks), 0) < count_ref[...], cols_ref[...], -1).astype(F32)
    raw = jnp.concatenate([raw, jnp.zeros((2 * GROUPS - slots_row, blocks), F32)], 0).astype(BF16)
    slot_row = iota((blocks, slots), 1) // slots_row
    spread = mm(raw, onehot(slot_row == iota((blocks, slots), 0)))[:slots_row, :]
    mine = iota((slots_row, slots), 1) % slots_row == iota((slots_row, slots), 0)
    cols = jnp.sum(jnp.where(mine, spread, 0.0), axis=0, keepdims=True)
    is_live = cols >= 0.0
    before = onehot(iota((slots, slots), 0) < iota((slots, slots), 1))
    counted = mm(jnp.broadcast_to(onehot(is_live), (16, slots)), before)[0:1, :]
    row_of = (iota((1, slots), 1) // slots_row).astype(F32)
    return row_of, cols, jnp.where(is_live, counted, -1.0)


def keep_live(compact, live):
    return onehot(iota((live, compact.shape[1]), 0).astype(F32) == compact)


def start_fetches(pairs, sems):
    fetches = [pltpu.make_async_copy(*pair, sems.at[i]) for i, pair in enumerate(pairs)]
    for fetch in fetches:
        fetch.start()
    return fetches


def prepare_kernel(copies, count_hbm, cols_hbm, dens_hbm, occ_hbm, t_hbm, *rest):
    outer = len(rest) - 16
    x_refs, (a_ref, table_ref, perm_hbm, perm_ref, count_ref, cols_ref, dens_ref, occ_ref, t_ref,
             rows_ref, xt_ref, flat, planes, lined, swapped, sems) = rest[:outer], rest[outer:]
    fetches = start_fetches(
        ((count_hbm, count_ref), (cols_hbm, cols_ref), (dens_hbm, dens_ref), (occ_hbm, occ_ref),
         (t_hbm, t_ref)),
        sems,
    )
    aux_dev, slots, _ = t_ref.shape
    live = table_ref.shape[1]
    blocks = cols_ref.shape[1]
    spread_tiles(perm_ref)
    keep_perm = pltpu.make_async_copy(perm_ref, perm_hbm, sems.at[5])
    keep_perm.start()
    for fetch in fetches[:4]:
        fetch.wait()
    occ = jnp.concatenate(
        [occ_ref[...].astype(F32), jnp.zeros((2 * GROUPS - 2, TILE), F32)], 0
    ).astype(BF16)
    own = as_rows(mm(occ, perm_ref[...]), rows_ref)
    row_of, cols, compact = index_slots(count_ref, cols_ref)
    keep = keep_live(compact, live)
    fetches[4].wait()
    for aux in range(aux_dev):
        swapped[aux * live : (aux + 1) * live, :] = mm(keep, t_ref[aux]).astype(BF16)
    flat[...] = mm(swapped[...], perm_ref[...])
    me = lax.axis_index("basis")
    for copy in range(copies):
        pack_columns(flat, xt_ref, aux_dev, 0, live, live // PACK, lambda n: (copy * BW + n) ^ me)
    height = xt_ref.shape[1]
    for far, x_ref in enumerate(x_refs):
        for near in range(NEAR):
            x_ref[near * height : (near + 1) * height, :] = xt_ref[far * NEAR + near]
        x_ref[NEAR * height :, :] = own

    sub = iota((LANES, slots), 0)
    facts = jnp.where(sub == 0, row_of, jnp.where(sub == 1, cols, 0.0)).astype(BF16)
    places = jnp.where(sub == 0, compact + 1.0, 0.0).astype(BF16)
    own_facts = mm_nt(keep, facts)
    own_row, own_col = own_facts[:, 0:1], own_facts[:, 1:2]
    block = iota((live, blocks), 1).astype(F32)
    own_table = mm_nt(facts, keep)[0:2, :].astype(I32)
    table_ref[0:1, :] = own_table[0:1, :] * (2 * BW)
    table_ref[1:2, :] = own_table[1:2, :] * (2 * LANES)
    turn = me % PACK
    part, rows = live // copies, live // PACK
    out_place = ((iota((1, live), 1) + live - me // BW * part) // (part // PACK) + turn) % PACK
    aux = aux_dev * len(x_refs) * NEAR
    virt_pick = []
    for j in range(2):
        partner = dens_ref[j : j + 1, :].astype(F32)
        col_partner, row_partner = (
            jnp.sum(jnp.where(place == block, partner, 0.0), axis=1, keepdims=True)
            for place in (own_col, own_row)
        )
        virt_pick.append(onehot((own_row == row_of) & (col_partner == cols)))
        occ_pick = onehot((row_partner == row_of) & (own_col == cols))
        found = mm_nt(places, occ_pick)[0:1, :].astype(I32) - 1
        source = jnp.maximum(found, 0)
        steps = (out_place * 2 + j + 3 * PACK - source // rows - turn) % PACK
        index = jnp.where(found < 0, PACK * rows, steps * rows + source % rows)
        table_ref[2 + j : 3 + j, :] = index * aux
    table_ref[4:8, :] = jnp.zeros((4, live), I32)
    lane = iota((LANES, LANES), 0)
    x = lane % BW
    within = onehot(
        iota((LANES, LANES), 1) == lane // BW * BW + (x % PACK) * GROUPS + x // PACK
    )
    for aux in range(aux_dev):
        for group in range(GROUPS):
            span = slice(group * LANES, (group + 1) * LANES)
            lined[:, span] = mm(t_ref[aux, :, span], within).astype(BF16)
        for j in range(2):
            gathered = mm(virt_pick[j], lined[...])
            for group in range(GROUPS):
                planes[pl.ds(j * live * 2 * GROUPS + aux * GROUPS + group, live, stride=2 * GROUPS), :] = (
                    gathered[:, group * LANES : (group + 1) * LANES]
                )
    if aux_dev == 1:
        for group in range(GROUPS):
            planes[pl.ds(GROUPS + group, 2 * live, stride=2 * GROUPS), :] = (
                jnp.zeros((2 * live, LANES), F32)
            )
    half = live * 2 * GROUPS
    for j in range(2):
        a_ref[:, j * LANES : (j + 1) * LANES] = planes[j * half : (j + 1) * half, :].astype(BF16)
    keep_perm.wait()


def virt_kernel(aux_dev, halves, table_hbm, dens_ref, a_ref, perm_hbm, xm_ref, token_ref,
                table_ref, perm_ref, weights, result, swapped, flat, sems):
    fetch_table, fetch_perm = start_fetches(((table_hbm, table_ref), (perm_hbm, perm_ref)), sems)
    live = table_ref.shape[1]
    token_ref[...] = jnp.zeros(token_ref.shape, F32)
    blocks, rows, _ = dens_ref.shape
    chunk = iota((GROUPS, LANES), 1) // BW

    def build(e, carry):
        tiles = dens_ref[e].astype(F32)
        for j in range(2):
            tile = tiles[j * GROUPS : (j + 1) * GROUPS, :]
            turned = [tile] + [pltpu.roll(tile, d * BW, 1) for d in range(1, PACK)]
            for i in range(PACK):
                for pair in range(PACK // 2):
                    both = [
                        jnp.where(chunk == i, turned[(i - inner) % PACK], 0.0)
                        for inner in (2 * pair, 2 * pair + 1)
                    ]
                    start = pl.multiple_of(e * 2 * LANES, 2 * LANES) + (
                        j * LANES + i * BW + pair * 2 * GROUPS
                    )
                    weights[pl.ds(start, 2 * GROUPS), :] = jnp.concatenate(both, 0).astype(BF16)
        return carry

    lax.fori_loop(0, blocks, build, 0, unroll=16)
    fetch_table.wait()

    def multiply(step, carry):
        for inner in range(128):
            s = step * 128 + inner
            start = pl.multiple_of(s * 2 * GROUPS, 2 * GROUPS)
            e = pl.multiple_of(table_ref[1, s], 2 * LANES)
            result[pl.ds(start, 2 * GROUPS), :] = mm(
                a_ref[pl.ds(start, 2 * GROUPS), :], weights[pl.ds(e, 2 * LANES), :]
            )
        return carry

    lax.fori_loop(0, live // 128, multiply, 0)
    for aux in range(aux_dev):
        for group in range(GROUPS):
            swapped[aux * live : (aux + 1) * live, group * LANES : (group + 1) * LANES] = (
                result[pl.ds(aux * GROUPS + group, live, stride=2 * GROUPS), :].astype(BF16)
            )
    fetch_perm.wait()
    flat[...] = mm(swapped[...], perm_ref[...])
    part = live // halves
    for half in range(halves):
        pack_columns(flat, xm_ref, aux_dev, half * part, live, part // PACK,
                     lambda n: half * BW + n)


def far_order(outer):
    return [0, outer - 1, *range(1, outer - 1)]


def regroup_kernel(token_ref, *refs):
    sources, targets = refs[:-NEAR], refs[-NEAR:]
    outer = len(sources)
    sources = [sources[far_order(outer).index(far)] for far in range(outer)]
    height = (sources[0].shape[0] - 2 * GROUPS) // NEAR
    for near, target in enumerate(targets):
        for far, source in enumerate(sources):
            target[far * height : (far + 1) * height, :] = (
                source[near * height : (near + 1) * height, :]
            )
            tiles = outer * height + far * 2 * GROUPS
            target[tiles : tiles + 2 * GROUPS, :] = source[NEAR * height :, :]


def by_slot(wide, aux_dev, rows, devices, r):
    return jnp.concatenate(
        [wide[pl.ds(aux * rows + r, devices, stride=aux_dev * rows), :] for aux in range(aux_dev)],
        0,
    )


def widen(source_ref, rows, wide):
    devices = source_ref.shape[0]
    for d in range(devices):
        wide[d * rows : (d + 1) * rows, :] = source_ref[d, :rows, :].astype(F32)


def occ_kernel(aux_dev, table_hbm, xm_ref, *rest):
    x_refs, (out_ref, table_ref, wide, planes, weights, held, wide_m, sem) = rest[:NEAR], rest[NEAR:]
    fetch_table = pltpu.make_async_copy(table_hbm, table_ref, sem)
    fetch_table.start()
    rows = table_ref.shape[1] // PACK
    height = aux_dev * rows
    outer = x_refs[0].shape[0] // (height + 2 * GROUPS)
    devices = outer * NEAR
    out_rows, aux = xm_ref.shape[1] // aux_dev, aux_dev * devices
    me = lax.axis_index("basis")
    for near, x_ref in enumerate(x_refs):
        for far in range(outer):
            owner = me ^ (far * NEAR + near)
            wide[pl.ds(pl.multiple_of(owner * height, height), height), :] = (
                x_ref[far * height : (far + 1) * height, :].astype(F32)
            )
            tiles = outer * height + far * 2 * GROUPS
            planes[pl.ds(pl.multiple_of(owner * 2 * GROUPS, 2 * GROUPS), 2 * GROUPS), :] = (
                x_ref[tiles : tiles + 2 * GROUPS, :].astype(F32)
            )
    chunk = iota((GROUPS, LANES), 1) // BW

    def build(tile_index, carry):
        tile = planes[pl.ds(pl.multiple_of(tile_index * GROUPS, GROUPS), GROUPS), :]
        turned = [tile] + [pltpu.roll(tile, d * BW, 1) for d in range(1, PACK)]
        copies = []
        for inner in range(PACK):
            copy = turned[-inner % PACK]
            for place in range(1, PACK):
                copy = jnp.where(chunk == place, turned[(place - inner) % PACK], copy)
            copies.append(copy)
        start = pl.multiple_of(tile_index * BW, BW)
        weights[pl.ds(start, BW), :] = jnp.concatenate(copies, 0).astype(BF16)
        return carry

    lax.fori_loop(0, 2 * devices, build, 0, unroll=32)
    widen(xm_ref, xm_ref.shape[1], wide_m)
    for r in range(rows):
        row = by_slot(wide, aux_dev, rows, devices, r)
        for steps in range(PACK):
            start = (steps * rows + r) * aux
            held[start : start + aux, :] = (
                pltpu.roll(row, steps * BW, 1) if steps else row
            ).astype(BF16)
    none = PACK * rows
    held[none * aux : (none + 1) * aux, :] = jnp.zeros((aux, LANES), BF16)
    in_chunk = [onehot(iota((aux, LANES), 1) // BW == place) for place in range(PACK)]
    of_chunk = [onehot(iota((2 * BW, LANES), 1) // BW == place) for place in range(PACK)]
    first = me // BW * (out_rows * PACK)
    bases = [first + (place + PACK - me % PACK) % PACK * out_rows for place in range(PACK)]
    fetch_table.wait()

    def multiply(r, total):
        parts, blocks = [], []
        for place in range(PACK):
            s = bases[place] + r
            for j in range(2):
                start = pl.multiple_of(table_ref[2 + j, s], aux)
                parts.append(held[pl.ds(start, aux), :] * in_chunk[(2 * place + j) % PACK])
            a = pl.multiple_of(table_ref[0, s], 2 * BW)
            blocks.append(weights[pl.ds(a, 2 * BW), :] * of_chunk[place])
        left = jnp.concatenate([sum(parts[1:PACK], parts[0]), sum(parts[PACK + 1 :], parts[PACK])], 1)
        m_occ = mm(left, jnp.concatenate(blocks, 0)).astype(BF16)
        m_virt = by_slot(wide_m, aux_dev, out_rows, devices, r).astype(BF16)
        return total + mm_nt(m_occ, m_virt)

    total = lax.fori_loop(0, out_rows, multiply, jnp.zeros((aux, aux), F32), unroll=32)
    out_ref[...] = jnp.concatenate(
        [total[aux_i * devices : (aux_i + 1) * devices, :] for aux_i in range(aux_dev)], 1
    )


def sum_kernel(aux_dev, part_ref, out_ref):
    devices, width = part_ref.shape
    aux = aux_dev * devices
    total = jnp.sum(part_ref[...], axis=0, keepdims=True)
    lane, col = iota((width, aux), 0), iota((width, aux), 1)
    for row in range(aux_dev):
        chosen = lane == row * aux + col % aux_dev * devices + col // aux_dev
        out_ref[row : row + 1, :] = jnp.dot(
            jnp.broadcast_to(total, (8, width)),
            jnp.where(chosen, 1.0, 0.0),
            precision=lax.Precision.HIGHEST,
            preferred_element_type=F32,
        )[0:1, :]


def is_hbm(out):
    return getattr(out, "memory_space", None) == pltpu.HBM


def call(kernel, outs, scratch, places, args, name, micros, mib=24):
    specs = {"v": pltpu.VMEM, "m": pltpu.VMEM, "a": pl.ANY, "h": pl.ANY}
    held = {"m": pltpu.VMEM, "a": pltpu.VMEM, "h": pltpu.HBM}
    args = [
        pltpu.with_memory_space_constraint(arg, held[place]) if place in held else arg
        for place, arg in zip(places, args)
    ]
    return pl.pallas_call(
        kernel,
        out_shape=outs,
        in_specs=[pl.BlockSpec(memory_space=specs[place]) for place in places],
        out_specs=jax.tree.map(
            lambda out: pl.BlockSpec(memory_space=pl.ANY if is_hbm(out) else pltpu.VMEM), outs
        ),
        scratch_shapes=scratch,
        compiler_params=pltpu.CompilerParams(vmem_limit_bytes=mib * 1024 * 1024),
        cost_estimate=pl.CostEstimate(
            flops=micros * 1_000_000_000, bytes_accessed=micros * 3_000_000, transcendentals=0
        ),
        name=name,
    )(*args)


def exchange(x):
    return lax.all_to_all(x, "basis", split_axis=0, concat_axis=0, tiled=True)


def permute(x, devices, step):
    return lax.ppermute(x, "basis", [(i, i ^ step) for i in range(devices)])


def body(devices, coulomb, occ_tiles, virt_tiles, tile_count, tile_col, dens_col):
    aux_dev, blocks, slots_row, _ = coulomb.shape
    slots = blocks * slots_row
    live = slots // 2
    halves = devices // BW
    aux = aux_dev * devices
    rows_t = live // PACK
    rows_m = live // halves // PACK
    shape, vmem, dma = jax.ShapeDtypeStruct, pltpu.VMEM, pltpu.SemaphoreType.DMA

    outer = devices // NEAR
    dens = call(
        format_kernel,
        shape((devices, 2 * GROUPS, LANES), BF16),
        [vmem((2, TILE), BF16), vmem((2 * GROUPS, LANES), F32), dma],
        "h",
        (virt_tiles.reshape(2, TILE),),
        "format",
        1,
    )
    dens = exchange(dens)
    height = aux_dev * rows_t
    *xt, gathered, table, perm = call(
        functools.partial(prepare_kernel, halves),
        (
            *[shape((NEAR * height + 2 * GROUPS, LANES), BF16)] * outer,
            vmem((live * 2 * GROUPS, 2 * LANES), BF16),
            vmem((8, live), I32),
            pltpu.HBM((TILE, TILE), BF16),
        ),
        [
            vmem((TILE, TILE), BF16),
            vmem((1, blocks), I32),
            vmem((slots_row, blocks), I32),
            vmem((2, blocks), I32),
            vmem((2, TILE), BF16),
            vmem((aux_dev, slots, TILE), BF16),
            vmem((2 * GROUPS, LANES), F32),
            vmem((devices, height, LANES), BF16),
            vmem((aux_dev * live, TILE), F32),
            vmem((live * 4 * GROUPS, LANES), F32),
            vmem((slots, TILE), BF16),
            vmem((aux_dev * live, TILE), BF16),
            dma((6,)),
        ],
        "hhhhh",
        (
            tile_count.reshape(1, blocks),
            tile_col.T,
            dens_col.T,
            occ_tiles.reshape(2, TILE),
            coulomb.reshape(aux_dev, slots, TILE),
        ),
        "prepare",
        5,
    )
    for far in range(1, outer):
        xt[far] = permute(xt[far], devices, far * NEAR)
    xm, token = call(
        functools.partial(virt_kernel, aux_dev, halves),
        (shape((devices, aux_dev * rows_m, LANES), BF16), vmem((8, LANES), F32)),
        [
            pltpu.SMEM((8, live), I32),
            vmem((TILE, TILE), BF16),
            vmem((blocks * 2 * LANES, LANES), BF16),
            vmem((live * 2 * GROUPS, LANES), F32),
            vmem((aux_dev * live, TILE), BF16),
            vmem((aux_dev * live, TILE), F32),
            dma((2,)),
        ],
        "avmh",
        (table, dens, gathered, perm),
        "virt",
        100,
    )
    xm = exchange(xm)
    xt = list(call(
        regroup_kernel,
        (shape((outer * (height + 2 * GROUPS), LANES), BF16),) * NEAR,
        [],
        "m" + "v" * outer,
        (token, *[xt[far] for far in far_order(outer)]),
        "regroup",
        9,
    ))
    for near in range(1, NEAR):
        xt[near] = permute(xt[near], devices, near)
    part = call(
        functools.partial(occ_kernel, aux_dev),
        shape((devices, aux_dev * aux), F32),
        [
            pltpu.SMEM((8, live), I32),
            vmem((devices * height, LANES), F32),
            vmem((devices * 2 * GROUPS, LANES), F32),
            vmem((devices * 2 * BW, LANES), BF16),
            vmem(((PACK * rows_t + 1) * aux, LANES), BF16),
            vmem((devices * aux_dev * rows_m, LANES), F32),
            dma,
        ],
        "av" + "v" * NEAR,
        (table, xm, *xt),
        "occ",
        1,
    )
    part = exchange(part)
    return call(
        functools.partial(sum_kernel, aux_dev), shape((aux_dev, aux), F32), [], "v", (part,), "total", 1
    )


def solution(mesh):
    in_specs = (
        P(("parts", "basis"), None, None, None),
        P(("parts", "basis"), None, None),
        P(("parts", "basis"), None, None),
        P(),
        P(),
        P(),
    )
    out_specs = P(("parts", "basis"), None)
    return jax.shard_map(
        functools.partial(body, mesh.shape["basis"]),
        mesh=mesh,
        in_specs=in_specs,
        out_specs=out_specs,
        check_vma=False,
    )
```

```python
import functools

import jax
import jax.numpy as jnp
from jax import lax
from jax.experimental import pallas as pl
from jax.experimental.pallas import tpu as pltpu
from jax.sharding import PartitionSpec as P

F32, BF16, I32 = jnp.float32, jnp.bfloat16, jnp.int32
BW = 32
TILE = BW * BW
LANES = 128
PACK = LANES // BW
GROUPS = TILE // LANES
NEAR = 8


def mm(a, b):
    return jnp.dot(a, b, preferred_element_type=F32)


def mm_nt(a, b):
    return lax.dot_general(a, b, (((1,), (1,)), ((), ())), preferred_element_type=F32)


def iota(shape, dim):
    return lax.broadcasted_iota(I32, shape, dim)


def onehot(mask):
    return jnp.where(mask, 1.0, 0.0).astype(BF16)


def spread_tiles(perm_ref):
    for step in range(GROUPS):
        row = iota((LANES, TILE), 0) + step * LANES
        col = iota((LANES, TILE), 1)
        x, y = row // BW, row % BW
        perm_ref[step * LANES : (step + 1) * LANES, :] = onehot(
            col == y * BW + (x % PACK) * GROUPS + x // PACK
        )


def pack_columns(flat, out_ref, aux_dev, first, per_aux, rows, device):
    chunk = iota((rows, LANES), 1) // BW
    for group in range(GROUPS):
        for aux in range(aux_dev):
            turned = []
            for q in range(PACK):
                begin = aux * per_aux + first + q * rows
                part = flat[begin : begin + rows, group * LANES : (group + 1) * LANES]
                turned.append(pltpu.roll(part, q * BW, 1) if q else part)
            for inner in range(PACK):
                picked = turned[-inner % PACK]
                for place in range(1, PACK):
                    picked = jnp.where(chunk == place, turned[(place - inner) % PACK], picked)
                out_ref[device(PACK * group + inner), aux * rows : (aux + 1) * rows, :] = (
                    picked.astype(BF16)
                )


def as_rows(tiles, rows_ref):
    for group in range(GROUPS):
        rows_ref[pl.ds(group, 2, stride=GROUPS), :] = tiles[0:2, group * LANES : (group + 1) * LANES]
    return rows_ref[...].astype(BF16)


def format_kernel(virt_hbm, out_ref, virt_ref, rows_ref, sem):
    fetch = pltpu.make_async_copy(virt_hbm, virt_ref, sem)
    fetch.start()
    fetch.wait()
    own = as_rows(virt_ref[...].astype(F32), rows_ref)
    for d in range(out_ref.shape[0]):
        out_ref[d] = own


def index_slots(count_ref, cols_ref):
    slots_row, blocks = cols_ref.shape
    slots = slots_row * blocks
    raw = jnp.where(iota((slots_row, blocks), 0) < count_ref[...], cols_ref[...], -1).astype(F32)
    raw = jnp.concatenate([raw, jnp.zeros((2 * GROUPS - slots_row, blocks), F32)], 0).astype(BF16)
    slot_row = iota((blocks, slots), 1) // slots_row
    spread = mm(raw, onehot(slot_row == iota((blocks, slots), 0)))[:slots_row, :]
    mine = iota((slots_row, slots), 1) % slots_row == iota((slots_row, slots), 0)
    cols = jnp.sum(jnp.where(mine, spread, 0.0), axis=0, keepdims=True)
    is_live = cols >= 0.0
    before = onehot(iota((slots, slots), 0) < iota((slots, slots), 1))
    counted = mm(jnp.broadcast_to(onehot(is_live), (16, slots)), before)[0:1, :]
    row_of = (iota((1, slots), 1) // slots_row).astype(F32)
    return row_of, cols, jnp.where(is_live, counted, -1.0)


def keep_live(compact, live):
    return onehot(iota((live, compact.shape[1]), 0).astype(F32) == compact)


def start_fetches(pairs, sems):
    fetches = [pltpu.make_async_copy(*pair, sems.at[i]) for i, pair in enumerate(pairs)]
    for fetch in fetches:
        fetch.start()
    return fetches


def prepare_kernel(copies, count_hbm, cols_hbm, dens_hbm, occ_hbm, t_hbm, *rest):
    outer = len(rest) - 16
    x_refs, (a_ref, table_ref, perm_hbm, perm_ref, count_ref, cols_ref, dens_ref, occ_ref, t_ref,
             rows_ref, xt_ref, flat, planes, lined, swapped, sems) = rest[:outer], rest[outer:]
    fetches = start_fetches(
        ((count_hbm, count_ref), (cols_hbm, cols_ref), (dens_hbm, dens_ref), (occ_hbm, occ_ref),
         (t_hbm, t_ref)),
        sems,
    )
    aux_dev, slots, _ = t_ref.shape
    live = table_ref.shape[1]
    blocks = cols_ref.shape[1]
    spread_tiles(perm_ref)
    keep_perm = pltpu.make_async_copy(perm_ref, perm_hbm, sems.at[5])
    keep_perm.start()
    for fetch in fetches[:4]:
        fetch.wait()
    occ = jnp.concatenate(
        [occ_ref[...].astype(F32), jnp.zeros((2 * GROUPS - 2, TILE), F32)], 0
    ).astype(BF16)
    own = as_rows(mm(occ, perm_ref[...]), rows_ref)
    row_of, cols, compact = index_slots(count_ref, cols_ref)
    keep = keep_live(compact, live)
    fetches[4].wait()
    for aux in range(aux_dev):
        swapped[aux * live : (aux + 1) * live, :] = mm(keep, t_ref[aux]).astype(BF16)
    flat[...] = mm(swapped[...], perm_ref[...])
    me = lax.axis_index("basis")
    for copy in range(copies):
        pack_columns(flat, xt_ref, aux_dev, 0, live, live // PACK, lambda n: (copy * BW + n) ^ me)
    height = xt_ref.shape[1]
    for far, x_ref in enumerate(x_refs):
        for near in range(NEAR):
            x_ref[near * height : (near + 1) * height, :] = xt_ref[far * NEAR + near]
        x_ref[NEAR * height :, :] = own

    sub = iota((LANES, slots), 0)
    facts = jnp.where(sub == 0, row_of, jnp.where(sub == 1, cols, 0.0)).astype(BF16)
    places = jnp.where(sub == 0, compact + 1.0, 0.0).astype(BF16)
    own_facts = mm_nt(keep, facts)
    own_row, own_col = own_facts[:, 0:1], own_facts[:, 1:2]
    block = iota((live, blocks), 1).astype(F32)
    own_table = mm_nt(facts, keep)[0:2, :].astype(I32)
    table_ref[0:1, :] = own_table[0:1, :] * (2 * BW)
    table_ref[1:2, :] = own_table[1:2, :] * (2 * LANES)
    turn = me % PACK
    part, rows = live // copies, live // PACK
    out_place = ((iota((1, live), 1) + live - me // BW * part) // (part // PACK) + turn) % PACK
    aux = aux_dev * len(x_refs) * NEAR
    virt_pick = []
    for j in range(2):
        partner = dens_ref[j : j + 1, :].astype(F32)
        col_partner, row_partner = (
            jnp.sum(jnp.where(place == block, partner, 0.0), axis=1, keepdims=True)
            for place in (own_col, own_row)
        )
        virt_pick.append(onehot((own_row == row_of) & (col_partner == cols)))
        occ_pick = onehot((row_partner == row_of) & (own_col == cols))
        found = mm_nt(places, occ_pick)[0:1, :].astype(I32) - 1
        source = jnp.maximum(found, 0)
        steps = (out_place * 2 + j + 3 * PACK - source // rows - turn) % PACK
        index = jnp.where(found < 0, PACK * rows, steps * rows + source % rows)
        table_ref[2 + j : 3 + j, :] = index * aux
    table_ref[4:8, :] = jnp.zeros((4, live), I32)
    lane = iota((LANES, LANES), 0)
    x = lane % BW
    within = onehot(
        iota((LANES, LANES), 1) == lane // BW * BW + (x % PACK) * GROUPS + x // PACK
    )
    for aux in range(aux_dev):
        for group in range(GROUPS):
            span = slice(group * LANES, (group + 1) * LANES)
            lined[:, span] = mm(t_ref[aux, :, span], within).astype(BF16)
        for j in range(2):
            gathered = mm(virt_pick[j], lined[...])
            for group in range(GROUPS):
                planes[pl.ds(j * live * 2 * GROUPS + aux * GROUPS + group, live, stride=2 * GROUPS), :] = (
                    gathered[:, group * LANES : (group + 1) * LANES]
                )
    if aux_dev == 1:
        for group in range(GROUPS):
            planes[pl.ds(GROUPS + group, 2 * live, stride=2 * GROUPS), :] = (
                jnp.zeros((2 * live, LANES), F32)
            )
    half = live * 2 * GROUPS
    for j in range(2):
        a_ref[:, j * LANES : (j + 1) * LANES] = planes[j * half : (j + 1) * half, :].astype(BF16)
    keep_perm.wait()


def virt_kernel(aux_dev, halves, table_hbm, dens_ref, a_ref, perm_hbm, xm_ref, token_ref,
                table_ref, perm_ref, weights, result, swapped, flat, sems):
    fetch_table, fetch_perm = start_fetches(((table_hbm, table_ref), (perm_hbm, perm_ref)), sems)
    live = table_ref.shape[1]
    token_ref[...] = jnp.zeros(token_ref.shape, F32)
    blocks, rows, _ = dens_ref.shape
    chunk = iota((GROUPS, LANES), 1) // BW

    def build(e, carry):
        tiles = dens_ref[e].astype(F32)
        for j in range(2):
            tile = tiles[j * GROUPS : (j + 1) * GROUPS, :]
            turned = [tile] + [pltpu.roll(tile, d * BW, 1) for d in range(1, PACK)]
            for i in range(PACK):
                for pair in range(PACK // 2):
                    both = [
                        jnp.where(chunk == i, turned[(i - inner) % PACK], 0.0)
                        for inner in (2 * pair, 2 * pair + 1)
                    ]
                    start = pl.multiple_of(e * 2 * LANES, 2 * LANES) + (
                        j * LANES + i * BW + pair * 2 * GROUPS
                    )
                    weights[pl.ds(start, 2 * GROUPS), :] = jnp.concatenate(both, 0).astype(BF16)
        return carry

    lax.fori_loop(0, blocks, build, 0, unroll=16)
    fetch_table.wait()

    def multiply(step, carry):
        for inner in range(128):
            s = step * 128 + inner
            start = pl.multiple_of(s * 2 * GROUPS, 2 * GROUPS)
            e = pl.multiple_of(table_ref[1, s], 2 * LANES)
            result[pl.ds(start, 2 * GROUPS), :] = mm(
                a_ref[pl.ds(start, 2 * GROUPS), :], weights[pl.ds(e, 2 * LANES), :]
            )
        return carry

    lax.fori_loop(0, live // 128, multiply, 0)
    for aux in range(aux_dev):
        for group in range(GROUPS):
            swapped[aux * live : (aux + 1) * live, group * LANES : (group + 1) * LANES] = (
                result[pl.ds(aux * GROUPS + group, live, stride=2 * GROUPS), :].astype(BF16)
            )
    fetch_perm.wait()
    flat[...] = mm(swapped[...], perm_ref[...])
    part = live // halves
    for half in range(halves):
        pack_columns(flat, xm_ref, aux_dev, half * part, live, part // PACK,
                     lambda n: half * BW + n)


def far_order(outer):
    return [0, outer - 1, *range(1, outer - 1)]


def regroup_kernel(token_ref, *refs):
    sources, targets = refs[:-NEAR], refs[-NEAR:]
    outer = len(sources)
    sources = [sources[far_order(outer).index(far)] for far in range(outer)]
    height = (sources[0].shape[0] - 2 * GROUPS) // NEAR
    for near, target in enumerate(targets):
        for far, source in enumerate(sources):
            target[far * height : (far + 1) * height, :] = (
                source[near * height : (near + 1) * height, :]
            )
            tiles = outer * height + far * 2 * GROUPS
            target[tiles : tiles + 2 * GROUPS, :] = source[NEAR * height :, :]


def by_slot(wide, aux_dev, rows, devices, r):
    return jnp.concatenate(
        [wide[pl.ds(aux * rows + r, devices, stride=aux_dev * rows), :] for aux in range(aux_dev)],
        0,
    )


def widen(source_ref, rows, wide):
    devices = source_ref.shape[0]
    for d in range(devices):
        wide[d * rows : (d + 1) * rows, :] = source_ref[d, :rows, :].astype(F32)


def rows_kernel(aux_dev, xm_ref, out_ref, wide):
    devices, height, _ = xm_ref.shape
    rows = height // aux_dev
    widen(xm_ref, height, wide)
    for r in range(rows):
        out_ref[r] = by_slot(wide, aux_dev, rows, devices, r).astype(BF16)


def occ_kernel(aux_dev, table_hbm, mv_ref, *rest):
    x_refs, (out_ref, table_ref, wide, planes, weights, held, sem) = rest[:NEAR], rest[NEAR:]
    fetch_table = pltpu.make_async_copy(table_hbm, table_ref, sem)
    fetch_table.start()
    rows = table_ref.shape[1] // PACK
    height = aux_dev * rows
    outer = x_refs[0].shape[0] // (height + 2 * GROUPS)
    devices = outer * NEAR
    out_rows, aux = mv_ref.shape[0], mv_ref.shape[1]
    me = lax.axis_index("basis")
    for near, x_ref in enumerate(x_refs):
        for far in range(outer):
            owner = me ^ (far * NEAR + near)
            wide[pl.ds(pl.multiple_of(owner * height, height), height), :] = (
                x_ref[far * height : (far + 1) * height, :].astype(F32)
            )
            tiles = outer * height + far * 2 * GROUPS
            planes[pl.ds(pl.multiple_of(owner * 2 * GROUPS, 2 * GROUPS), 2 * GROUPS), :] = (
                x_ref[tiles : tiles + 2 * GROUPS, :].astype(F32)
            )
    chunk = iota((GROUPS, LANES), 1) // BW

    def build(tile_index, carry):
        tile = planes[pl.ds(pl.multiple_of(tile_index * GROUPS, GROUPS), GROUPS), :]
        turned = [tile] + [pltpu.roll(tile, d * BW, 1) for d in range(1, PACK)]
        copies = []
        for inner in range(PACK):
            copy = turned[-inner % PACK]
            for place in range(1, PACK):
                copy = jnp.where(chunk == place, turned[(place - inner) % PACK], copy)
            copies.append(copy)
        start = pl.multiple_of(tile_index * BW, BW)
        weights[pl.ds(start, BW), :] = jnp.concatenate(copies, 0).astype(BF16)
        return carry

    lax.fori_loop(0, 2 * devices, build, 0, unroll=32)
    for r in range(rows):
        row = by_slot(wide, aux_dev, rows, devices, r)
        for steps in range(PACK):
            start = (steps * rows + r) * aux
            held[start : start + aux, :] = (
                pltpu.roll(row, steps * BW, 1) if steps else row
            ).astype(BF16)
    none = PACK * rows
    held[none * aux : (none + 1) * aux, :] = jnp.zeros((aux, LANES), BF16)
    in_chunk = [onehot(iota((aux, LANES), 1) // BW == place) for place in range(PACK)]
    of_chunk = [onehot(iota((2 * BW, LANES), 1) // BW == place) for place in range(PACK)]
    first = me // BW * (out_rows * PACK)
    bases = [first + (place + PACK - me % PACK) % PACK * out_rows for place in range(PACK)]
    fetch_table.wait()

    def multiply(r, total):
        parts, blocks = [], []
        for place in range(PACK):
            s = bases[place] + r
            for j in range(2):
                start = pl.multiple_of(table_ref[2 + j, s], aux)
                parts.append(held[pl.ds(start, aux), :] * in_chunk[(2 * place + j) % PACK])
            a = pl.multiple_of(table_ref[0, s], 2 * BW)
            blocks.append(weights[pl.ds(a, 2 * BW), :] * of_chunk[place])
        left = jnp.concatenate([sum(parts[1:PACK], parts[0]), sum(parts[PACK + 1 :], parts[PACK])], 1)
        m_occ = mm(left, jnp.concatenate(blocks, 0)).astype(BF16)
        return total + mm_nt(m_occ, mv_ref[r])

    total = lax.fori_loop(0, out_rows, multiply, jnp.zeros((aux, aux), F32), unroll=32)
    out_ref[...] = jnp.concatenate(
        [total[aux_i * devices : (aux_i + 1) * devices, :] for aux_i in range(aux_dev)], 1
    )


def sum_kernel(aux_dev, part_ref, out_ref):
    devices, width = part_ref.shape
    aux = aux_dev * devices
    total = jnp.sum(part_ref[...], axis=0, keepdims=True)
    lane, col = iota((width, aux), 0), iota((width, aux), 1)
    for row in range(aux_dev):
        chosen = lane == row * aux + col % aux_dev * devices + col // aux_dev
        out_ref[row : row + 1, :] = jnp.dot(
            jnp.broadcast_to(total, (8, width)),
            jnp.where(chosen, 1.0, 0.0),
            precision=lax.Precision.HIGHEST,
            preferred_element_type=F32,
        )[0:1, :]


def is_hbm(out):
    return getattr(out, "memory_space", None) == pltpu.HBM


def call(kernel, outs, scratch, places, args, name, micros, mib=24):
    specs = {"v": pltpu.VMEM, "m": pltpu.VMEM, "a": pl.ANY, "h": pl.ANY}
    held = {"m": pltpu.VMEM, "a": pltpu.VMEM, "h": pltpu.HBM}
    args = [
        pltpu.with_memory_space_constraint(arg, held[place]) if place in held else arg
        for place, arg in zip(places, args)
    ]
    return pl.pallas_call(
        kernel,
        out_shape=outs,
        in_specs=[pl.BlockSpec(memory_space=specs[place]) for place in places],
        out_specs=jax.tree.map(
            lambda out: pl.BlockSpec(memory_space=pl.ANY if is_hbm(out) else pltpu.VMEM), outs
        ),
        scratch_shapes=scratch,
        compiler_params=pltpu.CompilerParams(vmem_limit_bytes=mib * 1024 * 1024),
        cost_estimate=pl.CostEstimate(
            flops=micros * 1_000_000_000, bytes_accessed=micros * 3_000_000, transcendentals=0
        ),
        name=name,
    )(*args)


def exchange(x):
    return lax.all_to_all(x, "basis", split_axis=0, concat_axis=0, tiled=True)


def permute(x, devices, step):
    return lax.ppermute(x, "basis", [(i, i ^ step) for i in range(devices)])


def body(devices, coulomb, occ_tiles, virt_tiles, tile_count, tile_col, dens_col):
    aux_dev, blocks, slots_row, _ = coulomb.shape
    slots = blocks * slots_row
    live = slots // 2
    halves = devices // BW
    aux = aux_dev * devices
    rows_t = live // PACK
    rows_m = live // halves // PACK
    shape, vmem, dma = jax.ShapeDtypeStruct, pltpu.VMEM, pltpu.SemaphoreType.DMA

    outer = devices // NEAR
    dens = call(
        format_kernel,
        shape((devices, 2 * GROUPS, LANES), BF16),
        [vmem((2, TILE), BF16), vmem((2 * GROUPS, LANES), F32), dma],
        "h",
        (virt_tiles.reshape(2, TILE),),
        "format",
        1,
    )
    dens = exchange(dens)
    height = aux_dev * rows_t
    *xt, gathered, table, perm = call(
        functools.partial(prepare_kernel, halves),
        (
            *[shape((NEAR * height + 2 * GROUPS, LANES), BF16)] * outer,
            vmem((live * 2 * GROUPS, 2 * LANES), BF16),
            vmem((8, live), I32),
            pltpu.HBM((TILE, TILE), BF16),
        ),
        [
            vmem((TILE, TILE), BF16),
            vmem((1, blocks), I32),
            vmem((slots_row, blocks), I32),
            vmem((2, blocks), I32),
            vmem((2, TILE), BF16),
            vmem((aux_dev, slots, TILE), BF16),
            vmem((2 * GROUPS, LANES), F32),
            vmem((devices, height, LANES), BF16),
            vmem((aux_dev * live, TILE), F32),
            vmem((live * 4 * GROUPS, LANES), F32),
            vmem((slots, TILE), BF16),
            vmem((aux_dev * live, TILE), BF16),
            dma((6,)),
        ],
        "hhhhh",
        (
            tile_count.reshape(1, blocks),
            tile_col.T,
            dens_col.T,
            occ_tiles.reshape(2, TILE),
            coulomb.reshape(aux_dev, slots, TILE),
        ),
        "prepare",
        5,
    )
    for far in range(1, outer):
        xt[far] = permute(xt[far], devices, far * NEAR)
    xm, token = call(
        functools.partial(virt_kernel, aux_dev, halves),
        (shape((devices, aux_dev * rows_m, LANES), BF16), vmem((8, LANES), F32)),
        [
            pltpu.SMEM((8, live), I32),
            vmem((TILE, TILE), BF16),
            vmem((blocks * 2 * LANES, LANES), BF16),
            vmem((live * 2 * GROUPS, LANES), F32),
            vmem((aux_dev * live, TILE), BF16),
            vmem((aux_dev * live, TILE), F32),
            dma((2,)),
        ],
        "avmh",
        (table, dens, gathered, perm),
        "virt",
        100,
    )
    xm = exchange(xm)
    xt = list(call(
        regroup_kernel,
        (shape((outer * (height + 2 * GROUPS), LANES), BF16),) * NEAR,
        [],
        "m" + "v" * outer,
        (token, *[xt[far] for far in far_order(outer)]),
        "regroup",
        9,
    ))
    for near in range(1, NEAR):
        xt[near] = permute(xt[near], devices, near)
    mv = call(
        functools.partial(rows_kernel, aux_dev),
        vmem((rows_m, aux, LANES), BF16),
        [vmem((devices * aux_dev * rows_m, LANES), F32)],
        "v",
        (xm,),
        "rows",
        1,
    )
    part = call(
        functools.partial(occ_kernel, aux_dev),
        shape((devices, aux_dev * aux), F32),
        [
            pltpu.SMEM((8, live), I32),
            vmem((devices * height, LANES), F32),
            vmem((devices * 2 * GROUPS, LANES), F32),
            vmem((devices * 2 * BW, LANES), BF16),
            vmem(((PACK * rows_t + 1) * aux, LANES), BF16),
            dma,
        ],
        "am" + "v" * NEAR,
        (table, mv, *xt),
        "occ",
        1,
    )
    part = exchange(part)
    return call(
        functools.partial(sum_kernel, aux_dev), shape((aux_dev, aux), F32), [], "v", (part,), "total", 1
    )


def solution(mesh):
    in_specs = (
        P(("parts", "basis"), None, None, None),
        P(("parts", "basis"), None, None),
        P(("parts", "basis"), None, None),
        P(),
        P(),
        P(),
    )
    out_specs = P(("parts", "basis"), None)
    return jax.shard_map(
        functools.partial(body, mesh.shape["basis"]),
        mesh=mesh,
        in_specs=in_specs,
        out_specs=out_specs,
        check_vma=False,
    )
```

```python
import functools

import jax
import jax.numpy as jnp
from jax import lax
from jax.experimental import pallas as pl
from jax.experimental.pallas import tpu as pltpu
from jax.sharding import PartitionSpec as P

F32, BF16, I32 = jnp.float32, jnp.bfloat16, jnp.int32
BW = 32
TILE = BW * BW
LANES = 128
PACK = LANES // BW
GROUPS = TILE // LANES
NEAR = 8
ORDER = (6, 4, 2, 7, 5, 3, 1, 0)


def mm(a, b):
    return jnp.dot(a, b, preferred_element_type=F32)


def mm_nt(a, b):
    return lax.dot_general(a, b, (((1,), (1,)), ((), ())), preferred_element_type=F32)


def iota(shape, dim):
    return lax.broadcasted_iota(I32, shape, dim)


def onehot(mask):
    return jnp.where(mask, 1.0, 0.0).astype(BF16)


def spread_tiles(perm_ref):
    for step in range(GROUPS):
        row = iota((LANES, TILE), 0) + step * LANES
        col = iota((LANES, TILE), 1)
        x, y = row // BW, row % BW
        perm_ref[step * LANES : (step + 1) * LANES, :] = onehot(
            col == y * BW + (x % PACK) * GROUPS + x // PACK
        )


def pack_columns(flat, out_ref, aux_dev, first, per_aux, rows, device):
    chunk = iota((rows, LANES), 1) // BW
    for group in range(GROUPS):
        for aux in range(aux_dev):
            turned = []
            for q in range(PACK):
                begin = aux * per_aux + first + q * rows
                part = flat[begin : begin + rows, group * LANES : (group + 1) * LANES]
                turned.append(pltpu.roll(part, q * BW, 1) if q else part)
            for inner in range(PACK):
                picked = turned[-inner % PACK]
                for place in range(1, PACK):
                    picked = jnp.where(chunk == place, turned[(place - inner) % PACK], picked)
                out_ref[device(PACK * group + inner), aux * rows : (aux + 1) * rows, :] = (
                    picked.astype(BF16)
                )


def as_rows(tiles, rows_ref):
    for group in range(GROUPS):
        rows_ref[pl.ds(group, 2, stride=GROUPS), :] = tiles[0:2, group * LANES : (group + 1) * LANES]
    return rows_ref[...].astype(BF16)


def format_kernel(virt_hbm, out_ref, virt_ref, rows_ref, sem):
    fetch = pltpu.make_async_copy(virt_hbm, virt_ref, sem)
    fetch.start()
    fetch.wait()
    own = as_rows(virt_ref[...].astype(F32), rows_ref)
    for d in range(out_ref.shape[0]):
        out_ref[d] = own


def index_slots(count_ref, cols_ref):
    slots_row, blocks = cols_ref.shape
    slots = slots_row * blocks
    raw = jnp.where(iota((slots_row, blocks), 0) < count_ref[...], cols_ref[...], -1).astype(F32)
    raw = jnp.concatenate([raw, jnp.zeros((2 * GROUPS - slots_row, blocks), F32)], 0).astype(BF16)
    slot_row = iota((blocks, slots), 1) // slots_row
    spread = mm(raw, onehot(slot_row == iota((blocks, slots), 0)))[:slots_row, :]
    mine = iota((slots_row, slots), 1) % slots_row == iota((slots_row, slots), 0)
    cols = jnp.sum(jnp.where(mine, spread, 0.0), axis=0, keepdims=True)
    is_live = cols >= 0.0
    before = onehot(iota((slots, slots), 0) < iota((slots, slots), 1))
    counted = mm(jnp.broadcast_to(onehot(is_live), (16, slots)), before)[0:1, :]
    row_of = (iota((1, slots), 1) // slots_row).astype(F32)
    return row_of, cols, jnp.where(is_live, counted, -1.0)


def keep_live(compact, live):
    return onehot(iota((live, compact.shape[1]), 0).astype(F32) == compact)


def start_fetches(pairs, sems):
    fetches = [pltpu.make_async_copy(*pair, sems.at[i]) for i, pair in enumerate(pairs)]
    for fetch in fetches:
        fetch.start()
    return fetches


def prepare_kernel(copies, count_hbm, cols_hbm, dens_hbm, occ_hbm, t_hbm, *rest):
    outer = len(rest) - 16
    x_refs, (a_ref, table_ref, perm_hbm, perm_ref, count_ref, cols_ref, dens_ref, occ_ref, t_ref,
             rows_ref, xt_ref, flat, planes, lined, swapped, sems) = rest[:outer], rest[outer:]
    fetches = start_fetches(
        ((count_hbm, count_ref), (cols_hbm, cols_ref), (dens_hbm, dens_ref), (occ_hbm, occ_ref),
         (t_hbm, t_ref)),
        sems,
    )
    aux_dev, slots, _ = t_ref.shape
    live = table_ref.shape[1]
    blocks = cols_ref.shape[1]
    spread_tiles(perm_ref)
    keep_perm = pltpu.make_async_copy(perm_ref, perm_hbm, sems.at[5])
    keep_perm.start()
    for fetch in fetches[:4]:
        fetch.wait()
    occ = jnp.concatenate(
        [occ_ref[...].astype(F32), jnp.zeros((2 * GROUPS - 2, TILE), F32)], 0
    ).astype(BF16)
    own = as_rows(mm(occ, perm_ref[...]), rows_ref)
    row_of, cols, compact = index_slots(count_ref, cols_ref)
    keep = keep_live(compact, live)
    fetches[4].wait()
    for aux in range(aux_dev):
        swapped[aux * live : (aux + 1) * live, :] = mm(keep, t_ref[aux]).astype(BF16)
    flat[...] = mm(swapped[...], perm_ref[...])
    me = lax.axis_index("basis")
    for copy in range(copies):
        pack_columns(flat, xt_ref, aux_dev, 0, live, live // PACK, lambda n: (copy * BW + n) ^ me)
    height = xt_ref.shape[1]
    for far, x_ref in enumerate(x_refs):
        for near in range(NEAR):
            x_ref[near * height : (near + 1) * height, :] = xt_ref[far * NEAR + near]
        x_ref[NEAR * height :, :] = own

    sub = iota((LANES, slots), 0)
    facts = jnp.where(sub == 0, row_of, jnp.where(sub == 1, cols, 0.0)).astype(BF16)
    places = jnp.where(sub == 0, compact + 1.0, 0.0).astype(BF16)
    own_facts = mm_nt(keep, facts)
    own_row, own_col = own_facts[:, 0:1], own_facts[:, 1:2]
    block = iota((live, blocks), 1).astype(F32)
    own_table = mm_nt(facts, keep)[0:2, :].astype(I32)
    table_ref[0:1, :] = own_table[0:1, :] * (2 * BW)
    table_ref[1:2, :] = own_table[1:2, :] * (2 * LANES)
    turn = me % PACK
    part, rows = live // copies, live // PACK
    out_place = ((iota((1, live), 1) + live - me // BW * part) // (part // PACK) + turn) % PACK
    aux = aux_dev * len(x_refs) * NEAR
    virt_pick = []
    for j in range(2):
        partner = dens_ref[j : j + 1, :].astype(F32)
        col_partner, row_partner = (
            jnp.sum(jnp.where(place == block, partner, 0.0), axis=1, keepdims=True)
            for place in (own_col, own_row)
        )
        virt_pick.append(onehot((own_row == row_of) & (col_partner == cols)))
        occ_pick = onehot((row_partner == row_of) & (own_col == cols))
        found = mm_nt(places, occ_pick)[0:1, :].astype(I32) - 1
        source = jnp.maximum(found, 0)
        steps = (out_place * 2 + j + 3 * PACK - source // rows - turn) % PACK
        index = jnp.where(found < 0, PACK * rows, steps * rows + source % rows)
        table_ref[2 + j : 3 + j, :] = index * aux
    table_ref[4:8, :] = jnp.zeros((4, live), I32)
    lane = iota((LANES, LANES), 0)
    x = lane % BW
    within = onehot(
        iota((LANES, LANES), 1) == lane // BW * BW + (x % PACK) * GROUPS + x // PACK
    )
    for aux in range(aux_dev):
        for group in range(GROUPS):
            span = slice(group * LANES, (group + 1) * LANES)
            lined[:, span] = mm(t_ref[aux, :, span], within).astype(BF16)
        for j in range(2):
            gathered = mm(virt_pick[j], lined[...])
            for group in range(GROUPS):
                planes[pl.ds(j * live * 2 * GROUPS + aux * GROUPS + group, live, stride=2 * GROUPS), :] = (
                    gathered[:, group * LANES : (group + 1) * LANES]
                )
    if aux_dev == 1:
        for group in range(GROUPS):
            planes[pl.ds(GROUPS + group, 2 * live, stride=2 * GROUPS), :] = (
                jnp.zeros((2 * live, LANES), F32)
            )
    half = live * 2 * GROUPS
    for j in range(2):
        a_ref[:, j * LANES : (j + 1) * LANES] = planes[j * half : (j + 1) * half, :].astype(BF16)
    keep_perm.wait()


def virt_kernel(aux_dev, halves, table_hbm, dens_ref, a_ref, perm_hbm, xm_ref, token_ref,
                table_ref, perm_ref, weights, result, swapped, flat, sems):
    fetch_table, fetch_perm = start_fetches(((table_hbm, table_ref), (perm_hbm, perm_ref)), sems)
    live = table_ref.shape[1]
    token_ref[...] = jnp.zeros(token_ref.shape, F32)
    blocks, rows, _ = dens_ref.shape
    chunk = iota((GROUPS, LANES), 1) // BW

    def build(e, carry):
        tiles = dens_ref[e].astype(F32)
        for j in range(2):
            tile = tiles[j * GROUPS : (j + 1) * GROUPS, :]
            turned = [tile] + [pltpu.roll(tile, d * BW, 1) for d in range(1, PACK)]
            for i in range(PACK):
                for pair in range(PACK // 2):
                    both = [
                        jnp.where(chunk == i, turned[(i - inner) % PACK], 0.0)
                        for inner in (2 * pair, 2 * pair + 1)
                    ]
                    start = pl.multiple_of(e * 2 * LANES, 2 * LANES) + (
                        j * LANES + i * BW + pair * 2 * GROUPS
                    )
                    weights[pl.ds(start, 2 * GROUPS), :] = jnp.concatenate(both, 0).astype(BF16)
        return carry

    lax.fori_loop(0, blocks, build, 0, unroll=16)
    fetch_table.wait()

    def multiply(step, carry):
        for inner in range(128):
            s = step * 128 + inner
            start = pl.multiple_of(s * 2 * GROUPS, 2 * GROUPS)
            e = pl.multiple_of(table_ref[1, s], 2 * LANES)
            result[pl.ds(start, 2 * GROUPS), :] = mm(
                a_ref[pl.ds(start, 2 * GROUPS), :], weights[pl.ds(e, 2 * LANES), :]
            )
        return carry

    lax.fori_loop(0, live // 128, multiply, 0)
    for aux in range(aux_dev):
        for group in range(GROUPS):
            swapped[aux * live : (aux + 1) * live, group * LANES : (group + 1) * LANES] = (
                result[pl.ds(aux * GROUPS + group, live, stride=2 * GROUPS), :].astype(BF16)
            )
    fetch_perm.wait()
    flat[...] = mm(swapped[...], perm_ref[...])
    part = live // halves
    for half in range(halves):
        pack_columns(flat, xm_ref, aux_dev, half * part, live, part // PACK,
                     lambda n: half * BW + n)


def far_order(outer):
    return [0, *range(2, outer), 1]


def regroup_kernel(token_ref, *refs):
    sources, targets = refs[:-NEAR], refs[-NEAR:]
    outer = len(sources)
    sources = [sources[far_order(outer).index(far)] for far in range(outer)]
    height = (sources[0].shape[0] - 2 * GROUPS) // NEAR
    for near, target in enumerate(targets):
        for far, source in enumerate(sources):
            target[far * height : (far + 1) * height, :] = (
                source[near * height : (near + 1) * height, :]
            )
            tiles = outer * height + far * 2 * GROUPS
            target[tiles : tiles + 2 * GROUPS, :] = source[NEAR * height :, :]


def by_slot(wide, aux_dev, rows, devices, r):
    return jnp.concatenate(
        [wide[pl.ds(aux * rows + r, devices, stride=aux_dev * rows), :] for aux in range(aux_dev)],
        0,
    )


def widen(source_ref, rows, wide):
    devices = source_ref.shape[0]
    for d in range(devices):
        wide[d * rows : (d + 1) * rows, :] = source_ref[d, :rows, :].astype(F32)


def rows_kernel(aux_dev, xm_ref, out_ref, wide):
    devices, height, _ = xm_ref.shape
    rows = height // aux_dev
    widen(xm_ref, height, wide)
    for r in range(rows):
        out_ref[r] = by_slot(wide, aux_dev, rows, devices, r).astype(BF16)


def occ_kernel(aux_dev, table_hbm, mv_ref, *rest):
    x_refs, (out_ref, table_ref, wide, planes, weights, held, sem) = rest[:NEAR], rest[NEAR:]
    fetch_table = pltpu.make_async_copy(table_hbm, table_ref, sem)
    fetch_table.start()
    rows = table_ref.shape[1] // PACK
    height = aux_dev * rows
    outer = x_refs[0].shape[0] // (height + 2 * GROUPS)
    devices = outer * NEAR
    out_rows, aux = mv_ref.shape[0], mv_ref.shape[1]
    me = lax.axis_index("basis")
    for near, x_ref in zip(ORDER, x_refs):
        for far in range(outer):
            owner = me ^ (far * NEAR + near)
            wide[pl.ds(pl.multiple_of(owner * height, height), height), :] = (
                x_ref[far * height : (far + 1) * height, :].astype(F32)
            )
            tiles = outer * height + far * 2 * GROUPS
            planes[pl.ds(pl.multiple_of(owner * 2 * GROUPS, 2 * GROUPS), 2 * GROUPS), :] = (
                x_ref[tiles : tiles + 2 * GROUPS, :].astype(F32)
            )
    chunk = iota((GROUPS, LANES), 1) // BW

    def build(tile_index, carry):
        tile = planes[pl.ds(pl.multiple_of(tile_index * GROUPS, GROUPS), GROUPS), :]
        turned = [tile] + [pltpu.roll(tile, d * BW, 1) for d in range(1, PACK)]
        copies = []
        for inner in range(PACK):
            copy = turned[-inner % PACK]
            for place in range(1, PACK):
                copy = jnp.where(chunk == place, turned[(place - inner) % PACK], copy)
            copies.append(copy)
        start = pl.multiple_of(tile_index * BW, BW)
        weights[pl.ds(start, BW), :] = jnp.concatenate(copies, 0).astype(BF16)
        return carry

    lax.fori_loop(0, 2 * devices, build, 0, unroll=32)
    for r in range(rows):
        row = by_slot(wide, aux_dev, rows, devices, r)
        for steps in range(PACK):
            start = (steps * rows + r) * aux
            held[start : start + aux, :] = (
                pltpu.roll(row, steps * BW, 1) if steps else row
            ).astype(BF16)
    none = PACK * rows
    held[none * aux : (none + 1) * aux, :] = jnp.zeros((aux, LANES), BF16)
    in_chunk = [onehot(iota((aux, LANES), 1) // BW == place) for place in range(PACK)]
    of_chunk = [onehot(iota((2 * BW, LANES), 1) // BW == place) for place in range(PACK)]
    first = me // BW * (out_rows * PACK)
    bases = [first + (place + PACK - me % PACK) % PACK * out_rows for place in range(PACK)]
    fetch_table.wait()

    def multiply(r, total):
        parts, blocks = [], []
        for place in range(PACK):
            s = bases[place] + r
            for j in range(2):
                start = pl.multiple_of(table_ref[2 + j, s], aux)
                parts.append(held[pl.ds(start, aux), :] * in_chunk[(2 * place + j) % PACK])
            a = pl.multiple_of(table_ref[0, s], 2 * BW)
            blocks.append(weights[pl.ds(a, 2 * BW), :] * of_chunk[place])
        left = jnp.concatenate([sum(parts[1:PACK], parts[0]), sum(parts[PACK + 1 :], parts[PACK])], 1)
        m_occ = mm(left, jnp.concatenate(blocks, 0)).astype(BF16)
        return total + mm_nt(m_occ, mv_ref[r])

    total = lax.fori_loop(0, out_rows, multiply, jnp.zeros((aux, aux), F32), unroll=32)
    out_ref[...] = jnp.concatenate(
        [total[aux_i * devices : (aux_i + 1) * devices, :] for aux_i in range(aux_dev)], 1
    )


def sum_kernel(aux_dev, part_ref, out_ref):
    devices, width = part_ref.shape
    aux = aux_dev * devices
    total = jnp.sum(part_ref[...], axis=0, keepdims=True)
    lane, col = iota((width, aux), 0), iota((width, aux), 1)
    for row in range(aux_dev):
        chosen = lane == row * aux + col % aux_dev * devices + col // aux_dev
        out_ref[row : row + 1, :] = jnp.dot(
            jnp.broadcast_to(total, (8, width)),
            jnp.where(chosen, 1.0, 0.0),
            precision=lax.Precision.HIGHEST,
            preferred_element_type=F32,
        )[0:1, :]


def is_hbm(out):
    return getattr(out, "memory_space", None) == pltpu.HBM


def call(kernel, outs, scratch, places, args, name, micros, mib=24):
    specs = {"v": pltpu.VMEM, "m": pltpu.VMEM, "a": pl.ANY, "h": pl.ANY}
    held = {"m": pltpu.VMEM, "a": pltpu.VMEM, "h": pltpu.HBM}
    args = [
        pltpu.with_memory_space_constraint(arg, held[place]) if place in held else arg
        for place, arg in zip(places, args)
    ]
    return pl.pallas_call(
        kernel,
        out_shape=outs,
        in_specs=[pl.BlockSpec(memory_space=specs[place]) for place in places],
        out_specs=jax.tree.map(
            lambda out: pl.BlockSpec(memory_space=pl.ANY if is_hbm(out) else pltpu.VMEM), outs
        ),
        scratch_shapes=scratch,
        compiler_params=pltpu.CompilerParams(vmem_limit_bytes=mib * 1024 * 1024),
        cost_estimate=pl.CostEstimate(
            flops=micros * 1_000_000_000, bytes_accessed=micros * 3_000_000, transcendentals=0
        ),
        name=name,
    )(*args)


def exchange(x):
    return lax.all_to_all(x, "basis", split_axis=0, concat_axis=0, tiled=True)


def permute(x, devices, step):
    return lax.ppermute(x, "basis", [(i, i ^ step) for i in range(devices)])


def body(devices, coulomb, occ_tiles, virt_tiles, tile_count, tile_col, dens_col):
    aux_dev, blocks, slots_row, _ = coulomb.shape
    slots = blocks * slots_row
    live = slots // 2
    halves = devices // BW
    aux = aux_dev * devices
    rows_t = live // PACK
    rows_m = live // halves // PACK
    shape, vmem, dma = jax.ShapeDtypeStruct, pltpu.VMEM, pltpu.SemaphoreType.DMA

    outer = devices // NEAR
    dens = call(
        format_kernel,
        shape((devices, 2 * GROUPS, LANES), BF16),
        [vmem((2, TILE), BF16), vmem((2 * GROUPS, LANES), F32), dma],
        "h",
        (virt_tiles.reshape(2, TILE),),
        "format",
        1,
    )
    dens = exchange(dens)
    height = aux_dev * rows_t
    *xt, gathered, table, perm = call(
        functools.partial(prepare_kernel, halves),
        (
            *[shape((NEAR * height + 2 * GROUPS, LANES), BF16)] * outer,
            vmem((live * 2 * GROUPS, 2 * LANES), BF16),
            vmem((8, live), I32),
            pltpu.HBM((TILE, TILE), BF16),
        ),
        [
            vmem((TILE, TILE), BF16),
            vmem((1, blocks), I32),
            vmem((slots_row, blocks), I32),
            vmem((2, blocks), I32),
            vmem((2, TILE), BF16),
            vmem((aux_dev, slots, TILE), BF16),
            vmem((2 * GROUPS, LANES), F32),
            vmem((devices, height, LANES), BF16),
            vmem((aux_dev * live, TILE), F32),
            vmem((live * 4 * GROUPS, LANES), F32),
            vmem((slots, TILE), BF16),
            vmem((aux_dev * live, TILE), BF16),
            dma((6,)),
        ],
        "hhhhh",
        (
            tile_count.reshape(1, blocks),
            tile_col.T,
            dens_col.T,
            occ_tiles.reshape(2, TILE),
            coulomb.reshape(aux_dev, slots, TILE),
        ),
        "prepare",
        5,
    )
    for far in range(1, outer):
        xt[far] = permute(xt[far], devices, far * NEAR)
    xm, token = call(
        functools.partial(virt_kernel, aux_dev, halves),
        (shape((devices, aux_dev * rows_m, LANES), BF16), vmem((8, LANES), F32)),
        [
            pltpu.SMEM((8, live), I32),
            vmem((TILE, TILE), BF16),
            vmem((blocks * 2 * LANES, LANES), BF16),
            vmem((live * 2 * GROUPS, LANES), F32),
            vmem((aux_dev * live, TILE), BF16),
            vmem((aux_dev * live, TILE), F32),
            dma((2,)),
        ],
        "avmh",
        (table, dens, gathered, perm),
        "virt",
        100,
    )
    xm = exchange(xm)
    xt = list(call(
        regroup_kernel,
        (shape((outer * (height + 2 * GROUPS), LANES), BF16),) * NEAR,
        [],
        "m" + "v" * outer,
        (token, *[xt[far] for far in far_order(outer)]),
        "regroup",
        9,
    ))
    xt = [permute(xt[near], devices, near) if near else xt[near] for near in ORDER]
    mv = call(
        functools.partial(rows_kernel, aux_dev),
        vmem((rows_m, aux, LANES), BF16),
        [vmem((devices * aux_dev * rows_m, LANES), F32)],
        "v",
        (xm,),
        "rows",
        1,
    )
    part = call(
        functools.partial(occ_kernel, aux_dev),
        shape((devices, aux_dev * aux), F32),
        [
            pltpu.SMEM((8, live), I32),
            vmem((devices * height, LANES), F32),
            vmem((devices * 2 * GROUPS, LANES), F32),
            vmem((devices * 2 * BW, LANES), BF16),
            vmem(((PACK * rows_t + 1) * aux, LANES), BF16),
            dma,
        ],
        "am" + "v" * NEAR,
        (table, mv, *xt),
        "occ",
        1,
    )
    part = exchange(part)
    return call(
        functools.partial(sum_kernel, aux_dev), shape((aux_dev, aux), F32), [], "v", (part,), "total", 1
    )


def solution(mesh):
    in_specs = (
        P(("parts", "basis"), None, None, None),
        P(("parts", "basis"), None, None),
        P(("parts", "basis"), None, None),
        P(),
        P(),
        P(),
    )
    out_specs = P(("parts", "basis"), None)
    return jax.shard_map(
        functools.partial(body, mesh.shape["basis"]),
        mesh=mesh,
        in_specs=in_specs,
        out_specs=out_specs,
        check_vma=False,
    )
```

```python
import functools

import jax
import jax.numpy as jnp
from jax import lax
from jax.experimental import pallas as pl
from jax.experimental.pallas import tpu as pltpu
from jax.sharding import PartitionSpec as P

F32, BF16, I32 = jnp.float32, jnp.bfloat16, jnp.int32
BW = 32
TILE = BW * BW
LANES = 128
PACK = LANES // BW
GROUPS = TILE // LANES
NEAR = 8
ORDER = (6, 4, 2, 5, 7, 3, 1, 0)


def mm(a, b):
    return jnp.dot(a, b, preferred_element_type=F32)


def mm_nt(a, b):
    return lax.dot_general(a, b, (((1,), (1,)), ((), ())), preferred_element_type=F32)


def iota(shape, dim):
    return lax.broadcasted_iota(I32, shape, dim)


def onehot(mask):
    return jnp.where(mask, 1.0, 0.0).astype(BF16)


def spread_tiles(perm_ref):
    for step in range(GROUPS):
        row = iota((LANES, TILE), 0) + step * LANES
        col = iota((LANES, TILE), 1)
        x, y = row // BW, row % BW
        perm_ref[step * LANES : (step + 1) * LANES, :] = onehot(
            col == y * BW + (x % PACK) * GROUPS + x // PACK
        )


def pack_columns(flat, out_ref, aux_dev, first, per_aux, rows, device):
    chunk = iota((rows, LANES), 1) // BW
    for group in range(GROUPS):
        for aux in range(aux_dev):
            turned = []
            for q in range(PACK):
                begin = aux * per_aux + first + q * rows
                part = flat[begin : begin + rows, group * LANES : (group + 1) * LANES]
                turned.append(pltpu.roll(part, q * BW, 1) if q else part)
            for inner in range(PACK):
                picked = turned[-inner % PACK]
                for place in range(1, PACK):
                    picked = jnp.where(chunk == place, turned[(place - inner) % PACK], picked)
                out_ref[device(PACK * group + inner), aux * rows : (aux + 1) * rows, :] = (
                    picked.astype(BF16)
                )


def as_rows(tiles, rows_ref):
    for group in range(GROUPS):
        rows_ref[pl.ds(group, 2, stride=GROUPS), :] = tiles[0:2, group * LANES : (group + 1) * LANES]
    return rows_ref[...].astype(BF16)


def format_kernel(virt_hbm, out_ref, virt_ref, rows_ref, sem):
    fetch = pltpu.make_async_copy(virt_hbm, virt_ref, sem)
    fetch.start()
    fetch.wait()
    own = as_rows(virt_ref[...].astype(F32), rows_ref)
    for d in range(out_ref.shape[0]):
        out_ref[d] = own


def index_slots(count_ref, cols_ref):
    slots_row, blocks = cols_ref.shape
    slots = slots_row * blocks
    raw = jnp.where(iota((slots_row, blocks), 0) < count_ref[...], cols_ref[...], -1).astype(F32)
    raw = jnp.concatenate([raw, jnp.zeros((2 * GROUPS - slots_row, blocks), F32)], 0).astype(BF16)
    slot_row = iota((blocks, slots), 1) // slots_row
    spread = mm(raw, onehot(slot_row == iota((blocks, slots), 0)))[:slots_row, :]
    mine = iota((slots_row, slots), 1) % slots_row == iota((slots_row, slots), 0)
    cols = jnp.sum(jnp.where(mine, spread, 0.0), axis=0, keepdims=True)
    is_live = cols >= 0.0
    before = onehot(iota((slots, slots), 0) < iota((slots, slots), 1))
    counted = mm(jnp.broadcast_to(onehot(is_live), (16, slots)), before)[0:1, :]
    row_of = (iota((1, slots), 1) // slots_row).astype(F32)
    return row_of, cols, jnp.where(is_live, counted, -1.0)


def keep_live(compact, live):
    return onehot(iota((live, compact.shape[1]), 0).astype(F32) == compact)


def start_fetches(pairs, sems):
    fetches = [pltpu.make_async_copy(*pair, sems.at[i]) for i, pair in enumerate(pairs)]
    for fetch in fetches:
        fetch.start()
    return fetches


def prepare_kernel(copies, count_hbm, cols_hbm, dens_hbm, occ_hbm, t_hbm, *rest):
    outer = len(rest) - 16
    x_refs, (a_ref, table_ref, perm_hbm, perm_ref, count_ref, cols_ref, dens_ref, occ_ref, t_ref,
             rows_ref, xt_ref, flat, planes, lined, swapped, sems) = rest[:outer], rest[outer:]
    fetches = start_fetches(
        ((count_hbm, count_ref), (cols_hbm, cols_ref), (dens_hbm, dens_ref), (occ_hbm, occ_ref),
         (t_hbm, t_ref)),
        sems,
    )
    aux_dev, slots, _ = t_ref.shape
    live = table_ref.shape[1]
    blocks = cols_ref.shape[1]
    spread_tiles(perm_ref)
    keep_perm = pltpu.make_async_copy(perm_ref, perm_hbm, sems.at[5])
    keep_perm.start()
    for fetch in fetches[:4]:
        fetch.wait()
    occ = jnp.concatenate(
        [occ_ref[...].astype(F32), jnp.zeros((2 * GROUPS - 2, TILE), F32)], 0
    ).astype(BF16)
    own = as_rows(mm(occ, perm_ref[...]), rows_ref)
    row_of, cols, compact = index_slots(count_ref, cols_ref)
    keep = keep_live(compact, live)
    fetches[4].wait()
    for aux in range(aux_dev):
        swapped[aux * live : (aux + 1) * live, :] = mm(keep, t_ref[aux]).astype(BF16)
    flat[...] = mm(swapped[...], perm_ref[...])
    me = lax.axis_index("basis")
    for copy in range(copies):
        pack_columns(flat, xt_ref, aux_dev, 0, live, live // PACK, lambda n: (copy * BW + n) ^ me)
    height = xt_ref.shape[1]
    for far, x_ref in enumerate(x_refs):
        for near in range(NEAR):
            x_ref[near * height : (near + 1) * height, :] = xt_ref[far * NEAR + near]
        x_ref[NEAR * height :, :] = own

    sub = iota((LANES, slots), 0)
    facts = jnp.where(sub == 0, row_of, jnp.where(sub == 1, cols, 0.0)).astype(BF16)
    places = jnp.where(sub == 0, compact + 1.0, 0.0).astype(BF16)
    own_facts = mm_nt(keep, facts)
    own_row, own_col = own_facts[:, 0:1], own_facts[:, 1:2]
    block = iota((live, blocks), 1).astype(F32)
    own_table = mm_nt(facts, keep)[0:2, :].astype(I32)
    table_ref[0:1, :] = own_table[0:1, :] * (2 * BW)
    table_ref[1:2, :] = own_table[1:2, :] * (2 * LANES)
    turn = me % PACK
    part, rows = live // copies, live // PACK
    out_place = ((iota((1, live), 1) + live - me // BW * part) // (part // PACK) + turn) % PACK
    aux = aux_dev * len(x_refs) * NEAR
    virt_pick = []
    for j in range(2):
        partner = dens_ref[j : j + 1, :].astype(F32)
        col_partner, row_partner = (
            jnp.sum(jnp.where(place == block, partner, 0.0), axis=1, keepdims=True)
            for place in (own_col, own_row)
        )
        virt_pick.append(onehot((own_row == row_of) & (col_partner == cols)))
        occ_pick = onehot((row_partner == row_of) & (own_col == cols))
        found = mm_nt(places, occ_pick)[0:1, :].astype(I32) - 1
        source = jnp.maximum(found, 0)
        steps = (out_place * 2 + j + 3 * PACK - source // rows - turn) % PACK
        index = jnp.where(found < 0, PACK * rows, steps * rows + source % rows)
        table_ref[2 + j : 3 + j, :] = index * aux
    table_ref[4:8, :] = jnp.zeros((4, live), I32)
    lane = iota((LANES, LANES), 0)
    x = lane % BW
    within = onehot(
        iota((LANES, LANES), 1) == lane // BW * BW + (x % PACK) * GROUPS + x // PACK
    )
    for aux in range(aux_dev):
        for group in range(GROUPS):
            span = slice(group * LANES, (group + 1) * LANES)
            lined[:, span] = mm(t_ref[aux, :, span], within).astype(BF16)
        for j in range(2):
            gathered = mm(virt_pick[j], lined[...])
            for group in range(GROUPS):
                planes[pl.ds(j * live * 2 * GROUPS + aux * GROUPS + group, live, stride=2 * GROUPS), :] = (
                    gathered[:, group * LANES : (group + 1) * LANES]
                )
    if aux_dev == 1:
        for group in range(GROUPS):
            planes[pl.ds(GROUPS + group, 2 * live, stride=2 * GROUPS), :] = (
                jnp.zeros((2 * live, LANES), F32)
            )
    half = live * 2 * GROUPS
    for j in range(2):
        a_ref[:, j * LANES : (j + 1) * LANES] = planes[j * half : (j + 1) * half, :].astype(BF16)
    keep_perm.wait()


def virt_kernel(aux_dev, halves, table_hbm, dens_ref, a_ref, perm_hbm, xm_ref, token_ref,
                table_ref, perm_ref, weights, result, swapped, flat, sems):
    fetch_table, fetch_perm = start_fetches(((table_hbm, table_ref), (perm_hbm, perm_ref)), sems)
    live = table_ref.shape[1]
    token_ref[...] = jnp.zeros(token_ref.shape, F32)
    blocks, rows, _ = dens_ref.shape
    chunk = iota((GROUPS, LANES), 1) // BW

    def build(e, carry):
        tiles = dens_ref[e].astype(F32)
        for j in range(2):
            tile = tiles[j * GROUPS : (j + 1) * GROUPS, :]
            turned = [tile] + [pltpu.roll(tile, d * BW, 1) for d in range(1, PACK)]
            for i in range(PACK):
                for pair in range(PACK // 2):
                    both = [
                        jnp.where(chunk == i, turned[(i - inner) % PACK], 0.0)
                        for inner in (2 * pair, 2 * pair + 1)
                    ]
                    start = pl.multiple_of(e * 2 * LANES, 2 * LANES) + (
                        j * LANES + i * BW + pair * 2 * GROUPS
                    )
                    weights[pl.ds(start, 2 * GROUPS), :] = jnp.concatenate(both, 0).astype(BF16)
        return carry

    lax.fori_loop(0, blocks, build, 0, unroll=16)
    fetch_table.wait()

    def multiply(step, carry):
        for inner in range(128):
            s = step * 128 + inner
            start = pl.multiple_of(s * 2 * GROUPS, 2 * GROUPS)
            e = pl.multiple_of(table_ref[1, s], 2 * LANES)
            result[pl.ds(start, 2 * GROUPS), :] = mm(
                a_ref[pl.ds(start, 2 * GROUPS), :], weights[pl.ds(e, 2 * LANES), :]
            )
        return carry

    lax.fori_loop(0, live // 128, multiply, 0)
    for aux in range(aux_dev):
        for group in range(GROUPS):
            swapped[aux * live : (aux + 1) * live, group * LANES : (group + 1) * LANES] = (
                result[pl.ds(aux * GROUPS + group, live, stride=2 * GROUPS), :].astype(BF16)
            )
    fetch_perm.wait()
    flat[...] = mm(swapped[...], perm_ref[...])
    part = live // halves
    for half in range(halves):
        pack_columns(flat, xm_ref, aux_dev, half * part, live, part // PACK,
                     lambda n: half * BW + n)


def far_order(outer):
    return [0, *range(2, outer), 1]


def regroup_kernel(token_ref, *refs):
    sources, targets = refs[:-NEAR], refs[-NEAR:]
    outer = len(sources)
    sources = [sources[far_order(outer).index(far)] for far in range(outer)]
    height = (sources[0].shape[0] - 2 * GROUPS) // NEAR
    for near, target in enumerate(targets):
        for far, source in enumerate(sources):
            target[far * height : (far + 1) * height, :] = (
                source[near * height : (near + 1) * height, :]
            )
            tiles = outer * height + far * 2 * GROUPS
            target[tiles : tiles + 2 * GROUPS, :] = source[NEAR * height :, :]


def by_slot(wide, aux_dev, rows, devices, r):
    return jnp.concatenate(
        [wide[pl.ds(aux * rows + r, devices, stride=aux_dev * rows), :] for aux in range(aux_dev)],
        0,
    )


def widen(source_ref, rows, wide):
    devices = source_ref.shape[0]
    for d in range(devices):
        wide[d * rows : (d + 1) * rows, :] = source_ref[d, :rows, :].astype(F32)


def rows_kernel(aux_dev, xm_ref, out_ref, wide):
    devices, height, _ = xm_ref.shape
    rows = height // aux_dev
    widen(xm_ref, height, wide)
    for r in range(rows):
        out_ref[r] = by_slot(wide, aux_dev, rows, devices, r).astype(BF16)


def occ_kernel(aux_dev, table_hbm, mv_ref, *rest):
    x_refs, (out_ref, table_ref, wide, planes, weights, held, sem) = rest[:NEAR], rest[NEAR:]
    fetch_table = pltpu.make_async_copy(table_hbm, table_ref, sem)
    fetch_table.start()
    rows = table_ref.shape[1] // PACK
    height = aux_dev * rows
    outer = x_refs[0].shape[0] // (height + 2 * GROUPS)
    devices = outer * NEAR
    out_rows, aux = mv_ref.shape[0], mv_ref.shape[1]
    me = lax.axis_index("basis")
    for near, x_ref in zip(ORDER, x_refs):
        for far in range(outer):
            owner = me ^ (far * NEAR + near)
            wide[pl.ds(pl.multiple_of(owner * height, height), height), :] = (
                x_ref[far * height : (far + 1) * height, :].astype(F32)
            )
            tiles = outer * height + far * 2 * GROUPS
            planes[pl.ds(pl.multiple_of(owner * 2 * GROUPS, 2 * GROUPS), 2 * GROUPS), :] = (
                x_ref[tiles : tiles + 2 * GROUPS, :].astype(F32)
            )
    chunk = iota((GROUPS, LANES), 1) // BW

    def build(tile_index, carry):
        tile = planes[pl.ds(pl.multiple_of(tile_index * GROUPS, GROUPS), GROUPS), :]
        turned = [tile] + [pltpu.roll(tile, d * BW, 1) for d in range(1, PACK)]
        copies = []
        for inner in range(PACK):
            copy = turned[-inner % PACK]
            for place in range(1, PACK):
                copy = jnp.where(chunk == place, turned[(place - inner) % PACK], copy)
            copies.append(copy)
        start = pl.multiple_of(tile_index * BW, BW)
        weights[pl.ds(start, BW), :] = jnp.concatenate(copies, 0).astype(BF16)
        return carry

    lax.fori_loop(0, 2 * devices, build, 0, unroll=32)
    for r in range(rows):
        row = by_slot(wide, aux_dev, rows, devices, r)
        for steps in range(PACK):
            start = (steps * rows + r) * aux
            held[start : start + aux, :] = (
                pltpu.roll(row, steps * BW, 1) if steps else row
            ).astype(BF16)
    none = PACK * rows
    held[none * aux : (none + 1) * aux, :] = jnp.zeros((aux, LANES), BF16)
    in_chunk = [onehot(iota((aux, LANES), 1) // BW == place) for place in range(PACK)]
    of_chunk = [onehot(iota((2 * BW, LANES), 1) // BW == place) for place in range(PACK)]
    first = me // BW * (out_rows * PACK)
    bases = [first + (place + PACK - me % PACK) % PACK * out_rows for place in range(PACK)]
    fetch_table.wait()

    def multiply(r, total):
        parts, blocks = [], []
        for place in range(PACK):
            s = bases[place] + r
            for j in range(2):
                start = pl.multiple_of(table_ref[2 + j, s], aux)
                parts.append(held[pl.ds(start, aux), :] * in_chunk[(2 * place + j) % PACK])
            a = pl.multiple_of(table_ref[0, s], 2 * BW)
            blocks.append(weights[pl.ds(a, 2 * BW), :] * of_chunk[place])
        left = jnp.concatenate([sum(parts[1:PACK], parts[0]), sum(parts[PACK + 1 :], parts[PACK])], 1)
        m_occ = mm(left, jnp.concatenate(blocks, 0)).astype(BF16)
        return total + mm_nt(m_occ, mv_ref[r])

    total = lax.fori_loop(0, out_rows, multiply, jnp.zeros((aux, aux), F32), unroll=32)
    out_ref[...] = jnp.concatenate(
        [total[aux_i * devices : (aux_i + 1) * devices, :] for aux_i in range(aux_dev)], 1
    )


def sum_kernel(aux_dev, part_ref, out_ref):
    devices, width = part_ref.shape
    aux = aux_dev * devices
    total = jnp.sum(part_ref[...], axis=0, keepdims=True)
    lane, col = iota((width, aux), 0), iota((width, aux), 1)
    for row in range(aux_dev):
        chosen = lane == row * aux + col % aux_dev * devices + col // aux_dev
        out_ref[row : row + 1, :] = jnp.dot(
            jnp.broadcast_to(total, (8, width)),
            jnp.where(chosen, 1.0, 0.0),
            precision=lax.Precision.HIGHEST,
            preferred_element_type=F32,
        )[0:1, :]


def is_hbm(out):
    return getattr(out, "memory_space", None) == pltpu.HBM


def call(kernel, outs, scratch, places, args, name, micros, mib=24):
    specs = {"v": pltpu.VMEM, "m": pltpu.VMEM, "a": pl.ANY, "h": pl.ANY}
    held = {"m": pltpu.VMEM, "a": pltpu.VMEM, "h": pltpu.HBM}
    args = [
        pltpu.with_memory_space_constraint(arg, held[place]) if place in held else arg
        for place, arg in zip(places, args)
    ]
    return pl.pallas_call(
        kernel,
        out_shape=outs,
        in_specs=[pl.BlockSpec(memory_space=specs[place]) for place in places],
        out_specs=jax.tree.map(
            lambda out: pl.BlockSpec(memory_space=pl.ANY if is_hbm(out) else pltpu.VMEM), outs
        ),
        scratch_shapes=scratch,
        compiler_params=pltpu.CompilerParams(vmem_limit_bytes=mib * 1024 * 1024),
        cost_estimate=pl.CostEstimate(
            flops=micros * 1_000_000_000, bytes_accessed=micros * 3_000_000, transcendentals=0
        ),
        name=name,
    )(*args)


def exchange(x):
    return lax.all_to_all(x, "basis", split_axis=0, concat_axis=0, tiled=True)


def permute(x, devices, step):
    return lax.ppermute(x, "basis", [(i, i ^ step) for i in range(devices)])


def body(devices, coulomb, occ_tiles, virt_tiles, tile_count, tile_col, dens_col):
    aux_dev, blocks, slots_row, _ = coulomb.shape
    slots = blocks * slots_row
    live = slots // 2
    halves = devices // BW
    aux = aux_dev * devices
    rows_t = live // PACK
    rows_m = live // halves // PACK
    shape, vmem, dma = jax.ShapeDtypeStruct, pltpu.VMEM, pltpu.SemaphoreType.DMA

    outer = devices // NEAR
    dens = call(
        format_kernel,
        shape((devices, 2 * GROUPS, LANES), BF16),
        [vmem((2, TILE), BF16), vmem((2 * GROUPS, LANES), F32), dma],
        "h",
        (virt_tiles.reshape(2, TILE),),
        "format",
        1,
    )
    dens = exchange(dens)
    height = aux_dev * rows_t
    *xt, gathered, table, perm = call(
        functools.partial(prepare_kernel, halves),
        (
            *[shape((NEAR * height + 2 * GROUPS, LANES), BF16)] * outer,
            vmem((live * 2 * GROUPS, 2 * LANES), BF16),
            vmem((8, live), I32),
            pltpu.HBM((TILE, TILE), BF16),
        ),
        [
            vmem((TILE, TILE), BF16),
            vmem((1, blocks), I32),
            vmem((slots_row, blocks), I32),
            vmem((2, blocks), I32),
            vmem((2, TILE), BF16),
            vmem((aux_dev, slots, TILE), BF16),
            vmem((2 * GROUPS, LANES), F32),
            vmem((devices, height, LANES), BF16),
            vmem((aux_dev * live, TILE), F32),
            vmem((live * 4 * GROUPS, LANES), F32),
            vmem((slots, TILE), BF16),
            vmem((aux_dev * live, TILE), BF16),
            dma((6,)),
        ],
        "hhhhh",
        (
            tile_count.reshape(1, blocks),
            tile_col.T,
            dens_col.T,
            occ_tiles.reshape(2, TILE),
            coulomb.reshape(aux_dev, slots, TILE),
        ),
        "prepare",
        5,
    )
    for far in range(1, outer):
        xt[far] = permute(xt[far], devices, far * NEAR)
    xm, token = call(
        functools.partial(virt_kernel, aux_dev, halves),
        (shape((devices, aux_dev * rows_m, LANES), BF16), vmem((8, LANES), F32)),
        [
            pltpu.SMEM((8, live), I32),
            vmem((TILE, TILE), BF16),
            vmem((blocks * 2 * LANES, LANES), BF16),
            vmem((live * 2 * GROUPS, LANES), F32),
            vmem((aux_dev * live, TILE), BF16),
            vmem((aux_dev * live, TILE), F32),
            dma((2,)),
        ],
        "avmh",
        (table, dens, gathered, perm),
        "virt",
        100,
    )
    xm = exchange(xm)
    xt = list(call(
        regroup_kernel,
        (shape((outer * (height + 2 * GROUPS), LANES), BF16),) * NEAR,
        [],
        "m" + "v" * outer,
        (token, *[xt[far] for far in far_order(outer)]),
        "regroup",
        9,
    ))
    xt = [permute(xt[near], devices, near) if near else xt[near] for near in ORDER]
    mv = call(
        functools.partial(rows_kernel, aux_dev),
        vmem((rows_m, aux, LANES), BF16),
        [vmem((devices * aux_dev * rows_m, LANES), F32)],
        "v",
        (xm,),
        "rows",
        1,
    )
    part = call(
        functools.partial(occ_kernel, aux_dev),
        shape((devices, aux_dev * aux), F32),
        [
            pltpu.SMEM((8, live), I32),
            vmem((devices * height, LANES), F32),
            vmem((devices * 2 * GROUPS, LANES), F32),
            vmem((devices * 2 * BW, LANES), BF16),
            vmem(((PACK * rows_t + 1) * aux, LANES), BF16),
            dma,
        ],
        "am" + "v" * NEAR,
        (table, mv, *xt),
        "occ",
        1,
    )
    part = exchange(part)
    return call(
        functools.partial(sum_kernel, aux_dev), shape((aux_dev, aux), F32), [], "v", (part,), "total", 1
    )


def solution(mesh):
    in_specs = (
        P(("parts", "basis"), None, None, None),
        P(("parts", "basis"), None, None),
        P(("parts", "basis"), None, None),
        P(),
        P(),
        P(),
    )
    out_specs = P(("parts", "basis"), None)
    return jax.shard_map(
        functools.partial(body, mesh.shape["basis"]),
        mesh=mesh,
        in_specs=in_specs,
        out_specs=out_specs,
        check_vma=False,
    )
```
